256 devices in a mesh: segment: 4 (over z_hi), mp: 16 (over y, x), dp: 4 (over z_lo, core).
Axes of the slice: x: 4, y: 4, z: 8 (z_hi: 4, z_lo: 2; z = z_hi * 2 + z_lo), core: 2. Of those that a mesh axis runs over, the one named last changes fastest.
Arguments:
- frames: bfloat16 [128, 128, 1536], P(('segment', 'dp'), 'mp'), may hold values from -6 to 6
- latent_init: bfloat16 [64, 1536], replicated, may hold values from -6 to 6
- norm_gains: bfloat16 [3, 1536], replicated, may hold values from 0.099609375 to 1.8984375
- res_query: bfloat16 [1536, 1536], P(None, 'mp'), may hold values from -0.15625 to 0.15625
- res_kv: bfloat16 [1536, 2, 1536], P(None, None, 'mp'), may hold values from -0.15625 to 0.15625
- res_out: bfloat16 [1536, 1536], replicated, may hold values from -0.15625 to 0.15625
- text: bfloat16 [4, 4, 768, 8192], P('segment', 'dp', None, 'mp'), may hold values from -6 to 6
- text_gain: bfloat16 [4, 8192], P('segment'), may hold values from 0.099609375 to 1.8984375
- w_query: bfloat16 [4, 8192, 8192], P('segment', 'dp', 'mp'), may hold values from -0.0625 to 0.0625
- w_kv: bfloat16 [4, 1536, 2, 8192], P('segment', 'dp', None, 'mp'), may hold values from -0.15625 to 0.15625
- xgate: float32 [4], P('segment'), may hold values from 0.3 to 1.2
- frame_counts: int32 [4, 4], P('segment', 'dp'), may hold values from 1 to 8
- frame_dest: int32 [128], replicated, may hold values from 0 to 127, each once
- cotangent: bfloat16 [4, 4, 768, 8192], P('segment', 'dp', None, 'mp'), may hold values from -6 to 6
Outputs:
- context: bfloat16 [4, 4, 768, 8192], P('segment', 'dp', None, 'mp')
- latent_grad: float32 [64, 128, 1536], P('mp', ('segment', 'dp'))
The draws below stay inside these ranges and needn't reach their ends.
Inputs may be any that keep to these rules, and one draw needn't show every extreme that they name: frame_dest is a permutation of the slots; a slot is used by its destination sequence only if its frame number is below that sequence's frame count.
All inputs are finite; a program needn't handle non-finite values.
Results may differ from the reference program's by a relative error of at most 0.04.
Values may be sent and summed in bfloat16 or wider, within the bound.
No kernel may reach another device: no remote copies, remote signals or barrier semaphores. Data moves between devices by JAX's collectives and lax.ppermute only.
A program may use at most 128 MiB of HBM per device.

```python
import math
import jax
import jax.numpy as jnp
from jax import lax

D = 8192
HEADS = 64
HD = 128
E = 1536
RHEADS = 16
RESAMPLE_HEAD_DIM = 96
LAT = 64
FMAX = 8
PATCH = 128
TXT = 768
SEQS = 4
SLOTS = 128
N_SEGMENT = 4


def touch_ends(result, own_key, low, high):
    longest = result.shape.index(max(result.shape))
    spots = []
    for shift in (0, 1):
        where = [jax.random.randint(jax.random.fold_in(own_key, axis), (), 0, length) for axis, length in enumerate(result.shape)]
        where[longest] = (where[longest] + shift) % result.shape[longest]
        spots.append(tuple(where))
    return result.at[spots[0]].set(low).at[spots[1]].set(high)


def levels(stream_key, extent, shards, low, top_value):
    loudness, own = 1.0, jax.random.fold_in(stream_key, 6)
    for position, parts in shards:
        steps = jnp.exp(jax.random.uniform(jax.random.fold_in(own, position), (parts,), jnp.float32, low / len(shards), top_value / len(shards)))
        loudness = loudness * jnp.repeat(steps, extent[position] // parts).reshape([-1 if axis == position else 1 for axis in range(len(extent))])
    return loudness


def gaussian(stream_key, dims, deviation, bound, split=(), held_as=jnp.bfloat16):
    gain = levels(stream_key, dims, split, -0.22, 0.18) if split else 1.0
    result = jax.random.normal(stream_key, dims, jnp.float32) * deviation * gain
    return jnp.minimum(jnp.maximum(result, -bound), bound).astype(held_as)


def setup_inputs(seed: int = 0) -> dict:
    splits = jax.random.split(jax.random.key(seed), 15)
    frames = gaussian(splits[0], (SLOTS, PATCH, E), 1.0, 6.0, ((0, 16), (1, 16)))
    latent_init = gaussian(splits[1], (LAT, E), 1.0, 6.0)
    norm_gains = jnp.clip(1.0 + 0.18 * jax.random.normal(splits[2], (3, E), jnp.float32), 0.099609375, 1.8984375).astype(jnp.bfloat16)
    res_query = gaussian(splits[3], (E, E), E ** -0.5, 0.15625, ((1, 16),))
    res_kv = gaussian(splits[4], (E, 2, E), E ** -0.5, 0.15625, ((2, 16),))
    res_out = gaussian(splits[5], (E, E), E ** -0.5, 0.15625)
    text = gaussian(splits[6], (N_SEGMENT, SEQS, TXT, D), 1.0, 6.0, ((0, 4), (1, 4), (3, 16)))
    text_gain = jnp.clip(1.0 + 0.18 * jax.random.normal(splits[7], (N_SEGMENT, D), jnp.float32), 0.099609375, 1.8984375).astype(jnp.bfloat16)
    w_query = gaussian(splits[8], (N_SEGMENT, D, D), D ** -0.5, 0.0625, ((0, 4), (1, 4), (2, 16)))
    w_kv = gaussian(splits[9], (N_SEGMENT, E, 2, D), E ** -0.5, 0.15625, ((0, 4), (1, 4), (3, 16)))
    xgate = jnp.clip(0.3 + 0.90000004 * jax.random.uniform(splits[10], (N_SEGMENT,), jnp.float32) ** levels(splits[10], (N_SEGMENT,), ((0, 4),), -0.2, 0.2), 0.3, 1.2)
    frame_counts = touch_ends(jax.random.randint(splits[11], (N_SEGMENT, SEQS), 1, FMAX + 1), jax.random.fold_in(splits[11], 1), 1, FMAX).astype(jnp.int32)
    frame_dest = jax.random.permutation(splits[12], SLOTS).astype(jnp.int32)
    cotangent = gaussian(splits[13], (N_SEGMENT, SEQS, TXT, D), 1.0, 6.0, ((0, 4), (1, 4), (3, 16)))
    return dict(frames=frames, latent_init=latent_init, norm_gains=norm_gains, res_query=res_query, res_kv=res_kv, res_out=res_out, text=text, text_gain=text_gain, w_query=w_query, w_kv=w_kv, xgate=xgate, frame_counts=frame_counts, frame_dest=frame_dest, cotangent=cotangent)


def layer_norm(inputs, gain_row):
    values = inputs.astype(jnp.float32)
    center = values - lax.optimization_barrier(jnp.mean(values, axis=-1, keepdims=True))
    spread = lax.optimization_barrier(jnp.mean(center * center, axis=-1, keepdims=True))
    return center * lax.rsqrt(spread + 1e-05) * gain_row.astype(jnp.float32)

def attend(query_matrix, key_value_block, live, gate):
    score_matrix = jnp.einsum('rag,lag->arl', query_matrix, key_value_block[:, 0], preferred_element_type=jnp.float32) / math.sqrt(query_matrix.shape[-1])
    score_matrix = jnp.where(live[None, None, :], score_matrix, -1e+30)
    row_max = lax.stop_gradient(lax.optimization_barrier(jnp.max(score_matrix, axis=-1, keepdims=True)))
    unnormalized_weights = jnp.exp(score_matrix - row_max)
    row_sum = lax.optimization_barrier(jnp.sum(unnormalized_weights, axis=-1))
    blended_values = jnp.einsum('lfv,vla->fla', unnormalized_weights.astype(jnp.bfloat16), key_value_block[:, 1], preferred_element_type=jnp.float32)
    blended_values = blended_values / jnp.transpose(row_sum)[:, :, None]
    return gate * blended_values.reshape(blended_values.shape[0], -1)

def reference(frames, latent_init, norm_gains, res_query, res_kv, res_out, text, text_gain, w_query, w_kv, xgate, frame_counts, frame_dest, cotangent):
    lat_norm = layer_norm(latent_init, norm_gains[1]).astype(jnp.bfloat16)
    resampler_heads = jnp.dot(lat_norm, res_query, preferred_element_type=jnp.float32).astype(jnp.bfloat16).reshape(LAT, RHEADS, RESAMPLE_HEAD_DIM)
    latent_pair_rows = jnp.einsum('le,ekc->lkc', lat_norm, res_kv, preferred_element_type=jnp.float32).astype(jnp.bfloat16).reshape(LAT, 2, RHEADS, RESAMPLE_HEAD_DIM)
    base_rows = latent_init.astype(jnp.float32)

    def resample_slot(slot_frames):
        media = layer_norm(slot_frames, norm_gains[0]).astype(jnp.bfloat16)
        media_pairs = jnp.einsum('pe,ekc->pkc', media, res_kv, preferred_element_type=jnp.float32).astype(jnp.bfloat16).reshape(PATCH, 2, RHEADS, RESAMPLE_HEAD_DIM)
        pair_list = jnp.concatenate([latent_pair_rows, media_pairs], axis=0)
        score_matrix = jnp.einsum('epg,apg->pea', resampler_heads, pair_list[:, 0], preferred_element_type=jnp.float32) / math.sqrt(RESAMPLE_HEAD_DIM)
        row_max = lax.optimization_barrier(jnp.max(score_matrix, axis=-1, keepdims=True))
        unnormalized_weights = jnp.exp(score_matrix - row_max)
        blended_values = jnp.einsum('oxq,qov->xov', unnormalized_weights.astype(jnp.bfloat16), pair_list[:, 1], preferred_element_type=jnp.float32)
        blended_values = blended_values / jnp.transpose(lax.optimization_barrier(jnp.sum(unnormalized_weights, axis=-1)))[:, :, None]
        res_context = blended_values.astype(jnp.bfloat16).reshape(LAT, RHEADS * RESAMPLE_HEAD_DIM)
        update = jnp.dot(res_context, res_out, preferred_element_type=jnp.float32)
        return layer_norm(base_rows + update, norm_gains[2]).astype(jnp.bfloat16)
    latents = lax.map(resample_slot, frames)
    slots = frame_dest.shape[0]
    owner = jnp.zeros((slots,), jnp.int32).at[frame_dest].set(jnp.arange(slots, dtype=jnp.int32))
    dest = latents[owner].reshape(N_SEGMENT, SEQS, FMAX * LAT, E)

    def segment_pass(operands):
        segment_text, gain_row, query_weight, pair_weight, gate_raw, counts, segment_dest, segment_cot = operands
        text_norm = layer_norm(segment_text, gain_row).astype(jnp.bfloat16).reshape(SEQS * TXT, D)
        query_matrix = jnp.dot(text_norm, query_weight, preferred_element_type=jnp.float32).astype(jnp.bfloat16).reshape(SEQS, TXT, HEADS, HD)
        pair_list = jnp.einsum('sme,ekc->smkc', segment_dest, pair_weight, preferred_element_type=jnp.float32).astype(jnp.bfloat16).reshape(SEQS, FMAX * LAT, 2, HEADS, HD)
        live = jnp.repeat(jnp.arange(FMAX, dtype=jnp.int32)[None, :] < counts[:, None], LAT, axis=1)
        gate = jnp.tanh(gate_raw.astype(jnp.float32))

        def local_attend(pair_in):
            return jax.vmap(attend, in_axes=(0, 0, 0, None))(query_matrix, pair_in, live, gate)
        gated, pull = jax.vjp(local_attend, pair_list)
        pair_grad, = pull(segment_cot.astype(jnp.float32))
        dest_grad = jnp.einsum('smkc,ekc->sme', pair_grad.reshape(SEQS, FMAX * LAT, 2, D).astype(jnp.float32), pair_weight.astype(jnp.float32), precision=lax.Precision.HIGHEST)
        return (gated.astype(jnp.bfloat16), dest_grad)
    context, dest_grad = lax.map(segment_pass, (text, text_gain, w_query, w_kv, xgate, frame_counts, dest, cotangent))
    grads_flat = dest_grad.reshape(slots, LAT, E)
    latent_grad = jnp.transpose(grads_flat[frame_dest], (1, 0, 2))
    return (context, latent_grad)
```

```python
import functools
import math

import jax
import jax.numpy as jnp
from jax import lax
from jax.experimental import pallas as pl
from jax.experimental.pallas import tpu as pltpu
from jax.sharding import PartitionSpec as P

HD = 128
E = 1536
RESAMPLE_HEAD_DIM = 96
LAT = 64
FMAX = 8
SIDE = 4
GROUP = ("segment", "dp")
BF16 = jnp.bfloat16
F32 = jnp.float32
VMEM_LIMIT = 56 * 1024 * 1024


def layer_norm(inputs, gain_row):
    values = inputs.astype(F32)
    center = values - jnp.mean(values, axis=-1, keepdims=True)
    spread = jnp.mean(center * center, axis=-1, keepdims=True)
    return center * lax.rsqrt(spread + 1e-05) * gain_row.astype(F32)


def shift(value, axis, by):
    pairs = []
    for i in range(SIDE * SIDE):
        y, x = divmod(i, SIDE)
        if axis == "x":
            x = (x + by) % SIDE
        else:
            y = (y + by) % SIDE
        pairs.append((i, y * SIDE + x))
    return lax.ppermute(value, "mp", pairs)


def ring(value, axis):
    half = value.shape[0] // 2
    left = shift(value, axis, 1)
    right = shift(value, axis, -1)
    far = jnp.concatenate([shift(left[:half], axis, 1), shift(right[half:], axis, -1)], axis=0)
    return [value, left, right, far]


def dp_blocks(value):
    over_z = lax.ppermute(value, "dp", [(0, 2), (1, 3), (2, 0), (3, 1)])
    mate = [(0, 1), (1, 0), (2, 3), (3, 2)]
    return [value, lax.ppermute(value, "dp", mate), over_z, lax.ppermute(over_z, "dp", mate)]


def query_kernel(where, text_ref, gain_ref, w0, w1, w2, w3, out_ref, normed):
    rows, depth = text_ref.shape
    width = 512

    @pl.loop(0, rows // 16)
    def _(step):
        at = pl.ds(pl.multiple_of(step * 16, 16), 16)
        total = jnp.zeros((16, width), F32)
        for c in range(depth // width):
            total += text_ref[at, c * width : (c + 1) * width].astype(F32)
        mean = jnp.sum(total, axis=1, keepdims=True) * (1.0 / depth)
        total = jnp.zeros((16, width), F32)
        for c in range(depth // width):
            center = text_ref[at, c * width : (c + 1) * width].astype(F32) - mean
            total += center * center
        spread = jnp.sum(total, axis=1, keepdims=True) * (1.0 / depth)
        scale = lax.rsqrt(spread + 1e-05)
        for c in range(depth // width):
            cols = slice(c * width, (c + 1) * width)
            center = text_ref[at, cols].astype(F32) - mean
            normed[at, cols] = (center * scale * gain_ref[:, cols].astype(F32)).astype(BF16)

    total = None
    for j, weight in enumerate((w0, w1, w2, w3)):
        block = weight.shape[0]
        cols = pl.ds(pl.multiple_of(where[j] * block, block), block)
        term = jnp.dot(normed[:, cols], weight[...], preferred_element_type=F32)
        total = term if total is None else total + term
    out_ref[...] = total.astype(BF16)


def query_matmul(text, gain, weights, where):
    tokens, depth = text.shape
    cols = weights[0].shape[1]
    rows = 128
    return pl.pallas_call(
        query_kernel,
        grid_spec=pltpu.PrefetchScalarGridSpec(
            num_scalar_prefetch=1,
            grid=(tokens // rows,),
            in_specs=[
                pl.BlockSpec((rows, depth), lambda i, w: (i, 0)),
                pl.BlockSpec((1, depth), lambda i, w: (0, 0)),
            ]
            + [pl.BlockSpec(w.shape, lambda i, w: (0, 0)) for w in weights],
            out_specs=pl.BlockSpec((rows, cols), lambda i, w: (i, 0)),
            scratch_shapes=[pltpu.VMEM((rows, depth), BF16)],
        ),
        out_shape=jax.ShapeDtypeStruct((tokens, cols), BF16),
        compiler_params=pltpu.CompilerParams(vmem_limit_bytes=VMEM_LIMIT),
    )(where, text, gain, *weights)


def attend_kernel(count, gate_ref, q_ref, k_ref, v_ref, cot_ref, ctx_ref, dk_ref, dv_ref, acc_k, acc_v):
    tokens = q_ref.shape[0]
    keys = k_ref.shape[0]
    rows = 256
    gate = gate_ref[0]
    slot = lax.broadcasted_iota(jnp.int32, (rows, keys), 1) % FMAX
    live = slot < count[0]
    across = (((1,), (1,)), ((), ()))
    down = (((0,), (0,)), ((), ()))
    for step in range(tokens // rows):
        at = slice(step * rows, (step + 1) * rows)
        q = q_ref[at, :]
        score = lax.dot_general(q, k_ref[...], across, preferred_element_type=F32)
        score = jnp.where(live, score * (1.0 / math.sqrt(HD)), -1e30)
        weight = jnp.exp(score - jnp.max(score, axis=1, keepdims=True))
        inverse = 1.0 / jnp.sum(weight, axis=1, keepdims=True)
        rounded = weight.astype(BF16)
        blend = jnp.dot(rounded, v_ref[...], preferred_element_type=F32) * inverse
        ctx_ref[at, :] = (gate * blend).astype(BF16)
        cot = gate * cot_ref[at, :].astype(F32)
        d_blend = (cot * inverse).astype(BF16)
        d_sum = -jnp.sum(cot * blend, axis=1, keepdims=True) * inverse
        d_weight = lax.dot_general(d_blend, v_ref[...], across, preferred_element_type=F32)
        d_weight = d_weight.astype(BF16).astype(F32) + d_sum
        d_score = (d_weight * weight * (1.0 / math.sqrt(HD))).astype(BF16)
        grad_k = lax.dot_general(d_score, q, down, preferred_element_type=F32)
        grad_v = lax.dot_general(rounded, d_blend, down, preferred_element_type=F32)
        if step == 0:
            acc_k[...] = grad_k
            acc_v[...] = grad_v
        else:
            acc_k[...] += grad_k
            acc_v[...] += grad_v
    dk_ref[...] = acc_k[...].astype(BF16)
    dv_ref[...] = acc_v[...].astype(BF16)


def attention(query, pairs, cot, count, gate):
    tokens, cols = query.shape
    keys = pairs.shape[0]
    heads = cols // HD
    head = lambda n: pl.BlockSpec((n, HD), lambda h, c: (0, h))
    return pl.pallas_call(
        attend_kernel,
        grid_spec=pltpu.PrefetchScalarGridSpec(
            num_scalar_prefetch=1,
            grid=(heads,),
            in_specs=[
                pl.BlockSpec(memory_space=pltpu.SMEM),
                head(tokens),
                head(keys),
                pl.BlockSpec((keys, HD), lambda h, c: (0, h + heads)),
                head(tokens),
            ],
            out_specs=[head(tokens), head(keys), head(keys)],
            scratch_shapes=[pltpu.VMEM((keys, HD), F32), pltpu.VMEM((keys, HD), F32)],
        ),
        out_shape=[
            jax.ShapeDtypeStruct((tokens, cols), BF16),
            jax.ShapeDtypeStruct((keys, cols), BF16),
            jax.ShapeDtypeStruct((keys, cols), BF16),
        ],
        compiler_params=pltpu.CompilerParams(vmem_limit_bytes=VMEM_LIMIT),
    )(count, gate, query, pairs, pairs, cot)


def per_device(
    frames,
    latent_init,
    norm_gains,
    res_query,
    res_kv,
    res_out,
    text,
    text_gain,
    w_query,
    w_kv,
    xgate,
    frame_counts,
    frame_dest,
    cotangent,
):
    mp_count = lax.axis_size("mp")
    group = lax.axis_index(GROUP)
    dp = lax.axis_index("dp")
    share = LAT // mp_count
    slots = frame_dest.shape[0]
    owned = frames.shape[0]
    groups = slots // owned
    width = res_query.shape[1]
    res_scale = 1.0 / math.sqrt(RESAMPLE_HEAD_DIM)

    whole_text = lax.all_gather(text[0, 0], "mp", axis=1, tiled=True)
    media = layer_norm(frames, norm_gains[0]).astype(BF16)
    half = owned // 2
    ring_x = [ring(media[:half], "x"), ring(media[half:], "y")]
    query_blocks = dp_blocks(w_query[0])
    kv_local = jnp.concatenate([w_kv[0, :, 0], w_kv[0, :, 1]], axis=1)
    kv_blocks = dp_blocks(kv_local)

    lat_norm = layer_norm(latent_init, norm_gains[1]).astype(BF16)
    res_pair = jnp.concatenate([res_kv[:, 0], res_kv[:, 1]], axis=1)
    res_q = jnp.dot(lat_norm, res_query, preferred_element_type=F32).astype(BF16)
    lat_pairs = jnp.dot(lat_norm, res_pair, preferred_element_type=F32).astype(BF16)
    media_halves = []
    for blocks, axis in zip(ring_x, ("y", "x")):
        joined = jnp.concatenate(blocks, axis=1)
        parts = [
            jnp.einsum("fpe,ec->fpc", block, res_pair, preferred_element_type=F32).astype(BF16)
            for block in ring(joined, axis)
        ]
        media_halves.append(jnp.concatenate(parts, axis=1))
    media_pairs = jnp.concatenate(media_halves, axis=0)
    pair_list = jnp.concatenate(
        [jnp.broadcast_to(lat_pairs, (owned,) + lat_pairs.shape), media_pairs], axis=1
    )
    score = (
        jnp.einsum("ld,fpd->flp", res_q, pair_list[:, :, :width], preferred_element_type=F32)
        * res_scale
    )
    weights = jnp.exp(score - jnp.max(score, axis=-1, keepdims=True))
    blend = jnp.einsum(
        "flp,fpd->fld", weights.astype(BF16), pair_list[:, :, width:], preferred_element_type=F32
    )
    res_context = (blend / jnp.sum(weights, axis=-1)[:, :, None]).astype(BF16)

    piece = res_context.reshape(owned, groups, share * width).swapaxes(0, 1)
    piece = lax.all_to_all(piece, GROUP, 0, 0, tiled=True).reshape(slots, share * width)
    slot_ids = jnp.arange(slots, dtype=jnp.int32)
    to_dest = (frame_dest[None, :] == slot_ids[:, None]).astype(BF16)
    piece = jnp.dot(to_dest, piece, preferred_element_type=F32).astype(BF16)
    piece = lax.all_to_all(
        piece.reshape(mp_count, owned, share * width), "mp", 0, 0, tiled=True
    )
    rows = piece.reshape(mp_count, owned, share, width).transpose(2, 1, 0, 3)
    update = jnp.einsum(
        "lfc,ce->lfe", rows.reshape(share, owned, E), res_out, preferred_element_type=F32
    )
    base_rows = lax.dynamic_slice_in_dim(latent_init, group * share, share, 0).astype(F32)
    latents = layer_norm(base_rows[:, None, :] + update, norm_gains[2]).astype(BF16)
    dp_count = lax.axis_size("dp")

    def place(g, m):
        return (g // dp_count * mp_count + m) * dp_count + g % dp_count

    mine = lax.ppermute(
        latents.reshape(share * owned, E),
        ("segment", "mp", "dp"),
        [(place(g, m), place(m, g)) for g in range(groups) for m in range(mp_count)],
    )
    dest = lax.all_to_all(
        jnp.broadcast_to(mine, (mp_count,) + mine.shape), "mp", 0, 0, tiled=True
    ).reshape(LAT * owned, E)

    where = jnp.stack([dp, dp ^ 1, dp ^ 2, dp ^ 3]).astype(jnp.int32)
    query = query_matmul(whole_text, text_gain, query_blocks, where)
    full_kv = jnp.zeros((E, kv_local.shape[1]), BF16)
    for j, block in enumerate(kv_blocks):
        full_kv = lax.dynamic_update_slice_in_dim(
            full_kv, block, where[j] * kv_local.shape[0], 0
        )
    pairs = jnp.dot(dest, full_kv, preferred_element_type=F32).astype(BF16)
    context, grad_k, grad_v = attention(
        query, pairs, cotangent[0, 0], frame_counts[0], jnp.tanh(xgate)
    )

    grad = jnp.concatenate([grad_k, grad_v], axis=1)
    part = lax.dot_general(
        grad, full_kv, (((1,), (1,)), ((), ())), preferred_element_type=F32
    ).astype(BF16)
    part = lax.all_to_all(part.reshape(mp_count, share * owned, E), "mp", 0, 0, tiled=True)
    dest_grad = jnp.sum(part.astype(F32), axis=0).astype(BF16)
    cut = groups // share
    send = (
        dest_grad.reshape(share, owned, cut, E // cut)
        .transpose(0, 2, 1, 3)
        .reshape(groups, owned, E // cut)
    )
    send = lax.all_to_all(send, GROUP, 0, 0, tiled=True).reshape(slots, E // cut)
    to_owner = (frame_dest[:, None] == slot_ids[None, :]).astype(BF16)
    send = jnp.dot(to_owner, send, preferred_element_type=F32).astype(BF16)
    send = lax.all_to_all(send.reshape(groups, owned, E // cut), GROUP, 0, 0, tiled=True)
    latent_grad = (
        send.reshape(share, cut, owned, E // cut)
        .transpose(0, 2, 1, 3)
        .reshape(share, owned, E)
        .astype(F32)
    )
    return (context[None, None], latent_grad)


def solution(mesh):
    in_specs = (
        P(("segment", "dp"), "mp", None),
        P(),
        P(),
        P(None, "mp"),
        P(None, None, "mp"),
        P(),
        P("segment", "dp", None, "mp"),
        P("segment", None),
        P("segment", "dp", "mp"),
        P("segment", "dp", None, "mp"),
        P("segment"),
        P("segment", "dp"),
        P(),
        P("segment", "dp", None, "mp"),
    )
    out_specs = (P("segment", "dp", None, "mp"), P("mp", ("segment", "dp"), None))
    return jax.shard_map(
        per_device, mesh=mesh, in_specs=in_specs, out_specs=out_specs, check_vma=False
    )
```

```python
import functools
import math

import jax
import jax.numpy as jnp
from jax import lax
from jax.experimental import pallas as pl
from jax.experimental.pallas import tpu as pltpu
from jax.sharding import PartitionSpec as P

HD = 128
E = 1536
RESAMPLE_HEAD_DIM = 96
LAT = 64
FMAX = 8
SIDE = 4
GROUP = ("segment", "dp")
BF16 = jnp.bfloat16
F32 = jnp.float32
VMEM_LIMIT = 56 * 1024 * 1024


def layer_norm(inputs, gain_row):
    values = inputs.astype(F32)
    center = values - jnp.mean(values, axis=-1, keepdims=True)
    spread = jnp.mean(center * center, axis=-1, keepdims=True)
    return center * lax.rsqrt(spread + 1e-05) * gain_row.astype(F32)


def shift(value, axis, by):
    pairs = []
    for i in range(SIDE * SIDE):
        y, x = divmod(i, SIDE)
        if axis == "x":
            x = (x + by) % SIDE
        else:
            y = (y + by) % SIDE
        pairs.append((i, y * SIDE + x))
    return lax.ppermute(value, "mp", pairs)


def ring(value, axis):
    half = value.shape[0] // 2
    left = shift(value, axis, 1)
    right = shift(value, axis, -1)
    far = jnp.concatenate([shift(left[:half], axis, 1), shift(right[half:], axis, -1)], axis=0)
    return [value, left, right, far]


def twice(k):
    return ((k << 1) ^ ((k >> 3) * 19)) & 15


def halved(k):
    return (k >> 1) ^ ((k & 1) * 9)


def dp_blocks(value):
    over_z = lax.ppermute(value, "dp", [(0, 2), (1, 3), (2, 0), (3, 1)])
    mate = [(0, 1), (1, 0), (2, 3), (3, 2)]
    return [value, lax.ppermute(value, "dp", mate), over_z, lax.ppermute(over_z, "dp", mate)]


def norm_kernel(value_ref, gain_ref, out_ref):
    out_ref[...] = layer_norm(value_ref[...], gain_ref[...]).astype(BF16)


def norm_rows(value, gain):
    return pl.pallas_call(
        norm_kernel, out_shape=jax.ShapeDtypeStruct(value.shape, BF16)
    )(value, gain)


def latent_kernel(piece_ref, weight_ref, base_ref, gain_ref, out_ref):
    width = RESAMPLE_HEAD_DIM
    share = piece_ref.shape[1] // width
    heads = weight_ref.shape[0] // width
    owned = piece_ref.shape[0] // heads
    piece = piece_ref[...].astype(F32)
    total = base_ref[...]
    for h in range(heads):
        rows = piece[h * owned : (h + 1) * owned]
        left = jnp.concatenate(
            [rows[:, j * width : (j + 1) * width] for j in range(share)], axis=0
        )
        total = total + jnp.dot(
            left.astype(BF16),
            weight_ref[h * width : (h + 1) * width, :],
            preferred_element_type=F32,
        )
    out_ref[...] = layer_norm(total, gain_ref[...]).astype(BF16)


def latent_rows(piece, weight, base, gain):
    return pl.pallas_call(
        latent_kernel,
        out_shape=jax.ShapeDtypeStruct(base.shape, BF16),
        compiler_params=pltpu.CompilerParams(vmem_limit_bytes=VMEM_LIMIT),
    )(piece, weight, base, gain)


def query_kernel(where, text_ref, gain_ref, *rest):
    weights, out_ref, mean_ref, scale_ref = rest[:-3], rest[-3], rest[-2], rest[-1]
    rows, depth = text_ref.shape
    width = 512

    @pl.loop(0, rows // 16)
    def _(step):
        at = pl.ds(pl.multiple_of(step * 16, 16), 16)
        first = text_ref[at, :width].astype(F32)
        origin = jnp.sum(first, axis=1, keepdims=True) * (1.0 / width)
        total = first - origin
        square = total * total
        for c in range(1, depth // width):
            off = text_ref[at, c * width : (c + 1) * width].astype(F32) - origin
            total += off
            square += off * off
        total = jnp.sum(total, axis=1, keepdims=True) * (1.0 / depth)
        square = jnp.sum(square, axis=1, keepdims=True) * (1.0 / depth)
        spread = jnp.maximum(square - total * total, 0.0)
        mean_ref[at, :] = jnp.broadcast_to(origin + total, (16, 128))
        scale_ref[at, :] = jnp.broadcast_to(lax.rsqrt(spread + 1e-05), (16, 128))

    mean = mean_ref[:, :1]
    scale = scale_ref[:, :1]
    total = None
    parts = len(weights) // 4
    block = weights[0].shape[0]
    for j, weight in enumerate(weights):
        at = (where[j // parts] * parts + j % parts) * block
        cols = pl.ds(pl.multiple_of(at, block), block)
        center = text_ref[:, cols].astype(F32) - mean
        normed = (center * scale * gain_ref[:, cols].astype(F32)).astype(BF16)
        term = jnp.dot(normed, weight[...], preferred_element_type=F32)
        total = term if total is None else total + term
    out_ref[...] = total.astype(BF16)


def query_matmul(text, gain, weights, where):
    tokens, depth = text.shape
    cols = weights[0].shape[1]
    rows = 256
    return pl.pallas_call(
        query_kernel,
        grid_spec=pltpu.PrefetchScalarGridSpec(
            num_scalar_prefetch=1,
            grid=(tokens // rows,),
            in_specs=[
                pl.BlockSpec((rows, depth), lambda i, w: (i, 0)),
                pl.BlockSpec((1, depth), lambda i, w: (0, 0)),
            ]
            + [pl.BlockSpec(w.shape, lambda i, w: (0, 0)) for w in weights],
            out_specs=pl.BlockSpec((rows, cols), lambda i, w: (i, 0)),
            scratch_shapes=[pltpu.VMEM((rows, 128), F32), pltpu.VMEM((rows, 128), F32)],
        ),
        out_shape=jax.ShapeDtypeStruct((tokens, cols), BF16),
        compiler_params=pltpu.CompilerParams(vmem_limit_bytes=VMEM_LIMIT),
    )(where, text, gain, *weights)


def attend_kernel(count, order, gate_ref, q_ref, k_ref, v_ref, cot_ref, ctx_ref, dk_ref, dv_ref, acc_k, acc_v):
    tokens = q_ref.shape[0]
    keys = k_ref.shape[0]
    rows = 256
    gate = gate_ref[0]
    slot = lax.broadcasted_iota(jnp.int32, (rows, keys), 1) % FMAX
    live = slot < count[0]
    across = (((1,), (1,)), ((), ()))
    down = (((0,), (0,)), ((), ()))
    for step in range(tokens // rows):
        at = slice(step * rows, (step + 1) * rows)
        q = q_ref[at, :]
        score = lax.dot_general(q, k_ref[...], across, preferred_element_type=F32)
        score = jnp.where(live, score * (1.0 / math.sqrt(HD)), -1e30)
        weight = jnp.exp(score - jnp.max(score, axis=1, keepdims=True))
        inverse = 1.0 / jnp.sum(weight, axis=1, keepdims=True)
        rounded = weight.astype(BF16)
        blend = jnp.dot(rounded, v_ref[...], preferred_element_type=F32) * inverse
        ctx_ref[at, :] = (gate * blend).astype(BF16)
        cot = gate * cot_ref[at, :].astype(F32)
        d_blend = (cot * inverse).astype(BF16)
        d_sum = -jnp.sum(cot * blend, axis=1, keepdims=True) * inverse
        d_weight = lax.dot_general(d_blend, v_ref[...], across, preferred_element_type=F32)
        d_weight = d_weight.astype(BF16).astype(F32) + d_sum
        d_score = (d_weight * weight * (1.0 / math.sqrt(HD))).astype(BF16)
        grad_k = lax.dot_general(d_score, q, down, preferred_element_type=F32)
        grad_v = lax.dot_general(rounded, d_blend, down, preferred_element_type=F32)
        if step == 0:
            acc_k[...] = grad_k
            acc_v[...] = grad_v
        else:
            acc_k[...] += grad_k
            acc_v[...] += grad_v
    chunks = order.shape[0]
    size = keys // chunks
    for j in range(chunks):
        to = pl.ds(pl.multiple_of(order[j] * size, size), size)
        dk_ref[to, :] = acc_k[j * size : (j + 1) * size, :].astype(BF16)
        dv_ref[to, :] = acc_v[j * size : (j + 1) * size, :].astype(BF16)


def attention(query, pairs, cot, count, order, gate):
    tokens, cols = query.shape
    keys = pairs.shape[0]
    heads = cols // HD
    head = lambda n: pl.BlockSpec((n, HD), lambda h, c, o: (0, h))
    return pl.pallas_call(
        attend_kernel,
        grid_spec=pltpu.PrefetchScalarGridSpec(
            num_scalar_prefetch=2,
            grid=(heads,),
            in_specs=[
                pl.BlockSpec(memory_space=pltpu.SMEM),
                head(tokens),
                head(keys),
                pl.BlockSpec((keys, HD), lambda h, c, o: (0, h + heads)),
                head(tokens),
            ],
            out_specs=[head(tokens), head(keys), head(keys)],
            scratch_shapes=[pltpu.VMEM((keys, HD), F32), pltpu.VMEM((keys, HD), F32)],
        ),
        out_shape=[
            jax.ShapeDtypeStruct((tokens, cols), BF16),
            jax.ShapeDtypeStruct((keys, cols), BF16),
            jax.ShapeDtypeStruct((keys, cols), BF16),
        ],
        compiler_params=pltpu.CompilerParams(vmem_limit_bytes=VMEM_LIMIT),
    )(count, order, gate, query, pairs, pairs, cot)


def per_device(
    frames,
    latent_init,
    norm_gains,
    res_query,
    res_kv,
    res_out,
    text,
    text_gain,
    w_query,
    w_kv,
    xgate,
    frame_counts,
    frame_dest,
    cotangent,
):
    mp_count = lax.axis_size("mp")
    group = lax.axis_index(GROUP)
    dp = lax.axis_index("dp")
    share = LAT // mp_count
    slots = frame_dest.shape[0]
    owned = frames.shape[0]
    groups = slots // owned
    width = res_query.shape[1]
    res_scale = 1.0 / math.sqrt(RESAMPLE_HEAD_DIM)

    split = (text.shape[2] // 3) * 2
    text_first = lax.all_gather(text[0, 0, :split], "mp", axis=1, tiled=True)
    text_last = lax.all_gather(text[0, 0, split:], "mp", axis=1, tiled=True)
    media = norm_rows(frames.reshape(-1, E), norm_gains[:1]).reshape(frames.shape)
    half = owned // 2
    ring_x = [ring(media[:half], "x"), ring(media[half:], "y")]
    kv_local = jnp.concatenate([w_kv[0, :, 0], w_kv[0, :, 1]], axis=1)
    kv_blocks = dp_blocks(kv_local)
    depth = w_query.shape[1] // 2
    query_low = dp_blocks(w_query[0, :depth])

    lat_norm = layer_norm(latent_init, norm_gains[1]).astype(BF16)
    res_pair = jnp.concatenate([res_kv[:, 0], res_kv[:, 1]], axis=1)
    res_q = jnp.dot(lat_norm, res_query, preferred_element_type=F32).astype(BF16)
    lat_pairs = jnp.dot(lat_norm, res_pair, preferred_element_type=F32).astype(BF16)
    media_halves = []
    for blocks, axis in zip(ring_x, ("y", "x")):
        joined = jnp.concatenate(blocks, axis=1)
        parts = [
            jnp.einsum("fpe,ec->fpc", block, res_pair, preferred_element_type=F32).astype(BF16)
            for block in ring(joined, axis)
        ]
        media_halves.append(jnp.concatenate(parts, axis=1))
    media_pairs = jnp.concatenate(media_halves, axis=0)
    pair_list = jnp.concatenate(
        [jnp.broadcast_to(lat_pairs, (owned,) + lat_pairs.shape), media_pairs], axis=1
    )
    score = (
        jnp.einsum("ld,fpd->flp", res_q, pair_list[:, :, :width], preferred_element_type=F32)
        * res_scale
    )
    weights = jnp.exp(score - jnp.max(score, axis=-1, keepdims=True))
    blend = jnp.einsum(
        "flp,fpd->fld", weights.astype(BF16), pair_list[:, :, width:], preferred_element_type=F32
    )
    res_context = (blend / jnp.sum(weights, axis=-1)[:, :, None]).astype(BF16)

    piece = res_context.reshape(owned, groups, share * width).swapaxes(0, 1)
    piece = lax.all_to_all(piece, GROUP, 0, 0, tiled=True).reshape(slots, share * width)
    piece, query_rest = lax.optimization_barrier((piece, w_query[0, depth:]))
    query_high = dp_blocks(query_rest)
    slot_ids = jnp.arange(slots, dtype=jnp.int32)
    target = (twice(group) ^ (slot_ids // owned)) * owned + slot_ids % owned
    to_dest = (frame_dest[None, :] == target[:, None]).astype(BF16)
    piece = jnp.dot(to_dest, piece, preferred_element_type=F32).astype(BF16)
    piece = lax.all_to_all(
        piece.reshape(mp_count, owned, share * width), "mp", 0, 0, tiled=True
    )
    base_rows = lax.dynamic_slice_in_dim(latent_init, group * share, share, 0).astype(F32)
    latents = latent_rows(
        piece.reshape(slots, share * width),
        res_out,
        jnp.repeat(base_rows, owned, axis=0),
        norm_gains[2:],
    )
    dp_count = lax.axis_size("dp")

    def place(g, m):
        return (g // dp_count * mp_count + m) * dp_count + g % dp_count

    mine = lax.ppermute(
        latents,
        ("segment", "mp", "dp"),
        [(place(g, m), place(twice(g) ^ m, m)) for g in range(groups) for m in range(mp_count)],
    )
    dest = lax.all_to_all(
        jnp.broadcast_to(mine, (mp_count,) + mine.shape), "mp", 0, 0, tiled=True
    ).reshape(LAT * owned, E)
    order = halved(group ^ jnp.arange(mp_count, dtype=jnp.int32))

    where = jnp.stack([dp, dp ^ 1, dp ^ 2, dp ^ 3]).astype(jnp.int32)
    query_blocks = [w for both in zip(query_low, query_high) for w in both]
    query_first = query_matmul(text_first, text_gain, query_blocks, where)
    dest, query_first = lax.optimization_barrier((dest, query_first))
    query_last = query_matmul(text_last, text_gain, query_blocks, where)
    full_kv = jnp.zeros((E, kv_local.shape[1]), BF16)
    for j, block in enumerate(kv_blocks):
        full_kv = lax.dynamic_update_slice_in_dim(
            full_kv, block, where[j] * kv_local.shape[0], 0
        )
    pairs = jnp.dot(dest, full_kv, preferred_element_type=F32).astype(BF16)
    context, grad_k, grad_v = attention(
        jnp.concatenate([query_first, query_last], axis=0),
        pairs,
        cotangent[0, 0],
        frame_counts[0],
        order,
        jnp.tanh(xgate),
    )

    grad = jnp.concatenate([grad_k, grad_v], axis=1)
    part = lax.dot_general(
        grad, full_kv, (((1,), (1,)), ((), ())), preferred_element_type=F32
    ).astype(BF16)
    part = lax.all_to_all(part.reshape(mp_count, share * owned, E), "mp", 0, 0, tiled=True)
    dest_grad = jnp.sum(part.astype(F32), axis=0).astype(BF16)
    cut = groups // share
    send = (
        dest_grad.reshape(share, owned, cut, E // cut)
        .transpose(0, 2, 1, 3)
        .reshape(groups, owned, E // cut)
    )
    send = lax.all_to_all(send, GROUP, 0, 0, tiled=True).reshape(slots, E // cut)
    to_owner = (frame_dest[:, None] == slot_ids[None, :]).astype(BF16)
    send = jnp.dot(to_owner, send, preferred_element_type=F32).astype(BF16)
    send = lax.all_to_all(send.reshape(groups, owned, E // cut), GROUP, 0, 0, tiled=True)
    latent_grad = (
        send.reshape(share, cut, owned, E // cut)
        .transpose(0, 2, 1, 3)
        .reshape(share, owned, E)
        .astype(F32)
    )
    return (context[None, None], latent_grad)


def solution(mesh):
    in_specs = (
        P(("segment", "dp"), "mp", None),
        P(),
        P(),
        P(None, "mp"),
        P(None, None, "mp"),
        P(),
        P("segment", "dp", None, "mp"),
        P("segment", None),
        P("segment", "dp", "mp"),
        P("segment", "dp", None, "mp"),
        P("segment"),
        P("segment", "dp"),
        P(),
        P("segment", "dp", None, "mp"),
    )
    out_specs = (P("segment", "dp", None, "mp"), P("mp", ("segment", "dp"), None))
    return jax.shard_map(
        per_device, mesh=mesh, in_specs=in_specs, out_specs=out_specs, check_vma=False
    )
```

```python
import functools
import math

import jax
import jax.numpy as jnp
from jax import lax
from jax.experimental import pallas as pl
from jax.experimental.pallas import tpu as pltpu
from jax.sharding import PartitionSpec as P

HD = 128
E = 1536
RESAMPLE_HEAD_DIM = 96
LAT = 64
FMAX = 8
SIDE = 4
GROUP = ("segment", "dp")
BF16 = jnp.bfloat16
F32 = jnp.float32
VMEM_LIMIT = 36 * 1024 * 1024


def layer_norm(inputs, gain_row):
    values = inputs.astype(F32)
    center = values - jnp.mean(values, axis=-1, keepdims=True)
    spread = jnp.mean(center * center, axis=-1, keepdims=True)
    return center * lax.rsqrt(spread + 1e-05) * gain_row.astype(F32)


def shift(value, axis, by):
    pairs = []
    for i in range(SIDE * SIDE):
        y, x = divmod(i, SIDE)
        if axis == "x":
            x = (x + by) % SIDE
        else:
            y = (y + by) % SIDE
        pairs.append((i, y * SIDE + x))
    return lax.ppermute(value, "mp", pairs)


def ring(value, axis):
    half = value.shape[0] // 2
    left = shift(value, axis, 1)
    right = shift(value, axis, -1)
    far = jnp.concatenate([shift(left[:half], axis, 1), shift(right[half:], axis, -1)], axis=0)
    return [value, left, right, far]


def twice(k):
    return ((k << 1) ^ ((k >> 3) * 19)) & 15


def halved(k):
    return (k >> 1) ^ ((k & 1) * 9)


def over_z(value):
    return lax.ppermute(value, "dp", [(0, 2), (1, 3), (2, 0), (3, 1)])


def dp_blocks(value, across):
    mate = [(0, 1), (1, 0), (2, 3), (3, 2)]
    return [value, lax.ppermute(value, "dp", mate), across, lax.ppermute(across, "dp", mate)]


def norm_kernel(value_ref, gain_ref, out_ref):
    out_ref[...] = layer_norm(value_ref[...], gain_ref[...]).astype(BF16)


def norm_rows(value, gain):
    return pl.pallas_call(
        norm_kernel, out_shape=jax.ShapeDtypeStruct(value.shape, BF16)
    )(value, gain)


def latent_kernel(piece_ref, weight_ref, base_ref, gain_ref, out_ref):
    width = RESAMPLE_HEAD_DIM
    share = piece_ref.shape[1] // width
    heads = weight_ref.shape[0] // width
    owned = piece_ref.shape[0] // heads
    piece = piece_ref[...].astype(F32)
    total = base_ref[...]
    for h in range(heads):
        rows = piece[h * owned : (h + 1) * owned]
        left = jnp.concatenate(
            [rows[:, j * width : (j + 1) * width] for j in range(share)], axis=0
        )
        total = total + jnp.dot(
            left.astype(BF16),
            weight_ref[h * width : (h + 1) * width, :],
            preferred_element_type=F32,
        )
    out_ref[...] = layer_norm(total, gain_ref[...]).astype(BF16)


def latent_rows(piece, weight, base, gain):
    return pl.pallas_call(
        latent_kernel,
        out_shape=jax.ShapeDtypeStruct(base.shape, BF16),
        compiler_params=pltpu.CompilerParams(vmem_limit_bytes=VMEM_LIMIT),
    )(piece, weight, base, gain)


def query_kernel(where, text_ref, gain_ref, *rest):
    weights, out_ref, mean_ref, scale_ref = rest[:-3], rest[-3], rest[-2], rest[-1]
    rows, depth = text_ref.shape
    width = 512

    @pl.loop(0, rows // 16)
    def _(step):
        at = pl.ds(pl.multiple_of(step * 16, 16), 16)
        first = text_ref[at, :width].astype(F32)
        origin = jnp.sum(first, axis=1, keepdims=True) * (1.0 / width)
        total = first - origin
        square = total * total
        for c in range(1, depth // width):
            off = text_ref[at, c * width : (c + 1) * width].astype(F32) - origin
            total += off
            square += off * off
        total = jnp.sum(total, axis=1, keepdims=True) * (1.0 / depth)
        square = jnp.sum(square, axis=1, keepdims=True) * (1.0 / depth)
        spread = jnp.maximum(square - total * total, 0.0)
        mean_ref[at, :] = jnp.broadcast_to(origin + total, (16, 128))
        scale_ref[at, :] = jnp.broadcast_to(lax.rsqrt(spread + 1e-05), (16, 128))

    mean = mean_ref[:, :1]
    scale = scale_ref[:, :1]
    total = None
    parts = len(weights) // 4
    block = weights[0].shape[0]
    for j, weight in enumerate(weights):
        at = (where[j // parts] * parts + j % parts) * block
        cols = pl.ds(pl.multiple_of(at, block), block)
        center = text_ref[:, cols].astype(F32) - mean
        normed = (center * scale * gain_ref[:, cols].astype(F32)).astype(BF16)
        term = jnp.dot(normed, weight[...], preferred_element_type=F32)
        total = term if total is None else total + term
    out_ref[...] = total.astype(BF16)


def query_matmul(text, gain, weights, where):
    tokens, depth = text.shape
    cols = weights[0].shape[1]
    rows = 256
    return pl.pallas_call(
        query_kernel,
        grid_spec=pltpu.PrefetchScalarGridSpec(
            num_scalar_prefetch=1,
            grid=(tokens // rows,),
            in_specs=[
                pl.BlockSpec((rows, depth), lambda i, w: (i, 0)),
                pl.BlockSpec((1, depth), lambda i, w: (0, 0)),
            ]
            + [
                pl.BlockSpec(w.shape, lambda i, w: (0, 0), pipeline_mode=pl.Buffered(1))
                for w in weights
            ],
            out_specs=pl.BlockSpec((rows, cols), lambda i, w: (i, 0)),
            scratch_shapes=[pltpu.VMEM((rows, 128), F32), pltpu.VMEM((rows, 128), F32)],
        ),
        out_shape=jax.ShapeDtypeStruct((tokens, cols), BF16),
        compiler_params=pltpu.CompilerParams(vmem_limit_bytes=VMEM_LIMIT),
    )(where, text, gain, *weights)


def attend_kernel(
    count, order, where, gate_ref, q_ref, cot_ref, dest_ref, kv0, kv1, kv2, kv3,
    ctx_ref, part_ref, grads, acc, pair,
):
    tokens = q_ref.shape[0]
    keys = dest_ref.shape[0]
    block = kv0.shape[0]
    rows = 256
    gate = gate_ref[0]
    head = pl.program_id(0)
    cols_k = pl.ds(pl.multiple_of(head * HD, HD), HD)
    cols_v = pl.ds(pl.multiple_of((head + pl.num_programs(0)) * HD, HD), HD)
    places = [pl.ds(pl.multiple_of(where[j] * block, block), block) for j in range(4)]
    kv = (kv0, kv1, kv2, kv3)
    across = (((1,), (1,)), ((), ()))
    down = (((0,), (0,)), ((), ()))
    total = None
    for place, weight in zip(places, kv):
        both = jnp.concatenate([weight[:, cols_k], weight[:, cols_v]], axis=1)
        term = jnp.dot(dest_ref[:, place], both, preferred_element_type=F32)
        total = term if total is None else total + term
    pair[...] = total.astype(BF16)
    slot = lax.broadcasted_iota(jnp.int32, (1, keys), 1) % FMAX
    bias = jnp.where(slot < count[0], 0.0, -1e30)
    scale = 1.0 / math.sqrt(HD)
    for step in range(tokens // rows):
        at = slice(step * rows, (step + 1) * rows)
        q = q_ref[at, :]
        score = lax.dot_general(q, pair[:, :HD], across, preferred_element_type=F32) + bias
        top = jnp.max(score, axis=1, keepdims=True)
        weight = jnp.exp((score - top) * scale)
        inverse = 1.0 / jnp.sum(weight, axis=1, keepdims=True)
        rounded = weight.astype(BF16)
        blend = jnp.dot(rounded, pair[:, HD:], preferred_element_type=F32) * inverse
        ctx_ref[at, :] = (gate * blend).astype(BF16)
        cot = gate * cot_ref[at, :].astype(F32)
        d_blend = (cot * inverse).astype(BF16)
        d_sum = -jnp.sum(cot * blend, axis=1, keepdims=True) * inverse
        d_weight = lax.dot_general(d_blend, pair[:, HD:], across, preferred_element_type=F32)
        d_score = ((d_weight + d_sum) * weight).astype(BF16)
        grad_k = lax.dot_general(d_score, q, down, preferred_element_type=F32)
        grad_v = lax.dot_general(rounded, d_blend, down, preferred_element_type=F32)
        if step == 0:
            acc[:, :HD] = grad_k
            acc[:, HD:] = grad_v
        else:
            acc[:, :HD] += grad_k
            acc[:, HD:] += grad_v
    chunks = order.shape[0]
    size = keys // chunks
    for j in range(chunks):
        to = pl.ds(pl.multiple_of(order[j] * size, size), size)
        at = slice(j * size, (j + 1) * size)
        grads[to, cols_k] = (acc[at, :HD] * scale).astype(BF16)
        grads[to, cols_v] = acc[at, HD:].astype(BF16)

    @pl.when(head == pl.num_programs(0) - 1)
    def _():
        for place, weight in zip(places, kv):
            part_ref[:, place] = lax.dot_general(
                grads[...], weight[...], across, preferred_element_type=F32
            ).astype(BF16)


def attention(query, dest, kv_blocks, cot, count, order, where, gate):
    tokens, cols = query.shape
    keys, width = dest.shape
    heads = cols // HD
    head = pl.BlockSpec((tokens, HD), lambda h, *_: (0, h))
    whole = lambda a: pl.BlockSpec(a.shape, lambda h, *_: (0, 0), pipeline_mode=pl.Buffered(1))
    return pl.pallas_call(
        attend_kernel,
        grid_spec=pltpu.PrefetchScalarGridSpec(
            num_scalar_prefetch=3,
            grid=(heads,),
            in_specs=[pl.BlockSpec(memory_space=pltpu.SMEM), head, head, whole(dest)]
            + [whole(w) for w in kv_blocks],
            out_specs=[head, pl.BlockSpec((keys, width), lambda h, *_: (0, 0))],
            scratch_shapes=[
                pltpu.VMEM((keys, 2 * cols), BF16),
                pltpu.VMEM((keys, 2 * HD), F32),
                pltpu.VMEM((keys, 2 * HD), BF16),
            ],
        ),
        out_shape=[
            jax.ShapeDtypeStruct((tokens, cols), BF16),
            jax.ShapeDtypeStruct((keys, width), BF16),
        ],
        compiler_params=pltpu.CompilerParams(vmem_limit_bytes=VMEM_LIMIT),
    )(count, order, where, gate, query, cot, dest, *kv_blocks)


def per_device(
    frames,
    latent_init,
    norm_gains,
    res_query,
    res_kv,
    res_out,
    text,
    text_gain,
    w_query,
    w_kv,
    xgate,
    frame_counts,
    frame_dest,
    cotangent,
):
    mp_count = lax.axis_size("mp")
    group = lax.axis_index(GROUP)
    dp = lax.axis_index("dp")
    share = LAT // mp_count
    slots = frame_dest.shape[0]
    owned = frames.shape[0]
    groups = slots // owned
    width = res_query.shape[1]
    res_scale = 1.0 / math.sqrt(RESAMPLE_HEAD_DIM)

    whole_text = lax.all_gather(text[0, 0], "mp", axis=1, tiled=True)
    media = norm_rows(frames.reshape(-1, E), norm_gains[:1]).reshape(frames.shape)
    half = owned // 2
    ring_x = [ring(media[:half], "x"), ring(media[half:], "y")]
    kv_local = jnp.concatenate([w_kv[0, :, 0], w_kv[0, :, 1]], axis=1)
    kv_across = over_z(kv_local)
    depth = w_query.shape[1] // 2
    low_across = over_z(w_query[0, :depth])

    lat_norm = layer_norm(latent_init, norm_gains[1]).astype(BF16)
    res_pair = jnp.concatenate([res_kv[:, 0], res_kv[:, 1]], axis=1)
    res_q = jnp.dot(lat_norm, res_query, preferred_element_type=F32).astype(BF16)
    lat_pairs = jnp.dot(lat_norm, res_pair, preferred_element_type=F32).astype(BF16)
    media_halves = []
    joined_halves = [jnp.concatenate(blocks, axis=1) for blocks in ring_x]
    joined_halves, kv_across = lax.optimization_barrier((joined_halves, kv_across))
    for joined, axis in zip(joined_halves, ("y", "x")):
        parts = [
            jnp.einsum("fpe,ec->fpc", block, res_pair, preferred_element_type=F32).astype(BF16)
            for block in ring(joined, axis)
        ]
        media_halves.append(jnp.concatenate(parts, axis=1))
    media_halves, low_across = lax.optimization_barrier((media_halves, low_across))
    media_pairs = jnp.concatenate(media_halves, axis=0)
    pair_list = jnp.concatenate(
        [jnp.broadcast_to(lat_pairs, (owned,) + lat_pairs.shape), media_pairs], axis=1
    )
    score = (
        jnp.einsum("ld,fpd->flp", res_q, pair_list[:, :, :width], preferred_element_type=F32)
        * res_scale
    )
    weights = jnp.exp(score - jnp.max(score, axis=-1, keepdims=True))
    blend = jnp.einsum(
        "flp,fpd->fld", weights.astype(BF16), pair_list[:, :, width:], preferred_element_type=F32
    )
    res_context = (blend / jnp.sum(weights, axis=-1)[:, :, None]).astype(BF16)

    piece = res_context.reshape(owned, groups, share * width).swapaxes(0, 1)
    piece = lax.all_to_all(piece, GROUP, 0, 0, tiled=True).reshape(slots, share * width)
    piece, query_rest = lax.optimization_barrier((piece, w_query[0, depth:]))
    query_high = dp_blocks(query_rest, over_z(query_rest))
    query_low = dp_blocks(w_query[0, :depth], low_across)
    kv_blocks = dp_blocks(kv_local, kv_across)
    slot_ids = jnp.arange(slots, dtype=jnp.int32)
    target = (twice(group) ^ (slot_ids // owned)) * owned + slot_ids % owned
    to_dest = (frame_dest[None, :] == target[:, None]).astype(BF16)
    piece = jnp.dot(to_dest, piece, preferred_element_type=F32).astype(BF16)
    piece = lax.all_to_all(
        piece.reshape(mp_count, owned, share * width), "mp", 0, 0, tiled=True
    )
    base_rows = lax.dynamic_slice_in_dim(latent_init, group * share, share, 0).astype(F32)
    latents = latent_rows(
        piece.reshape(slots, share * width),
        res_out,
        jnp.repeat(base_rows, owned, axis=0),
        norm_gains[2:],
    )
    dp_count = lax.axis_size("dp")

    def place(g, m):
        return (g // dp_count * mp_count + m) * dp_count + g % dp_count

    mine = lax.ppermute(
        latents,
        ("segment", "mp", "dp"),
        [(place(g, m), place(twice(g) ^ m, m)) for g in range(groups) for m in range(mp_count)],
    )
    dest = lax.all_to_all(
        jnp.broadcast_to(mine, (mp_count,) + mine.shape), "mp", 0, 0, tiled=True
    ).reshape(LAT * owned, E)
    order = halved(group ^ jnp.arange(mp_count, dtype=jnp.int32))

    where = jnp.stack([dp, dp ^ 1, dp ^ 2, dp ^ 3]).astype(jnp.int32)
    query_blocks = [w for both in zip(query_low, query_high) for w in both]
    query = query_matmul(whole_text, text_gain, query_blocks, where)
    dest, query = lax.optimization_barrier((dest, query))
    context, part = attention(
        query, dest, kv_blocks, cotangent[0, 0], frame_counts[0], order, where, jnp.tanh(xgate)
    )

    part = lax.all_to_all(part.reshape(mp_count, share * owned, E), "mp", 0, 0, tiled=True)
    dest_grad = jnp.sum(part.astype(F32), axis=0).astype(BF16)
    cut = groups // share
    send = (
        dest_grad.reshape(share, owned, cut, E // cut)
        .transpose(0, 2, 1, 3)
        .reshape(groups, owned, E // cut)
    )
    send = lax.all_to_all(send, GROUP, 0, 0, tiled=True).reshape(slots, E // cut)
    to_owner = (frame_dest[:, None] == slot_ids[None, :]).astype(BF16)
    send = jnp.dot(to_owner, send, preferred_element_type=F32).astype(BF16)
    send = lax.all_to_all(send.reshape(groups, owned, E // cut), GROUP, 0, 0, tiled=True)
    latent_grad = (
        send.reshape(share, cut, owned, E // cut)
        .transpose(0, 2, 1, 3)
        .reshape(share, owned, E)
        .astype(F32)
    )
    return (context[None, None], latent_grad)


def solution(mesh):
    in_specs = (
        P(("segment", "dp"), "mp", None),
        P(),
        P(),
        P(None, "mp"),
        P(None, None, "mp"),
        P(),
        P("segment", "dp", None, "mp"),
        P("segment", None),
        P("segment", "dp", "mp"),
        P("segment", "dp", None, "mp"),
        P("segment"),
        P("segment", "dp"),
        P(),
        P("segment", "dp", None, "mp"),
    )
    out_specs = (P("segment", "dp", None, "mp"), P("mp", ("segment", "dp"), None))
    return jax.shard_map(
        per_device, mesh=mesh, in_specs=in_specs, out_specs=out_specs, check_vma=False
    )
```

```python
import functools
import math

import jax
import jax.numpy as jnp
from jax import lax
from jax.experimental import pallas as pl
from jax.experimental.pallas import tpu as pltpu
from jax.sharding import PartitionSpec as P

HD = 128
E = 1536
RESAMPLE_HEAD_DIM = 96
LAT = 64
FMAX = 8
SIDE = 4
GROUP = ("segment", "dp")
BF16 = jnp.bfloat16
F32 = jnp.float32
VMEM_LIMIT = 36 * 1024 * 1024


def layer_norm(inputs, gain_row):
    values = inputs.astype(F32)
    center = values - jnp.mean(values, axis=-1, keepdims=True)
    spread = jnp.mean(center * center, axis=-1, keepdims=True)
    return center * lax.rsqrt(spread + 1e-05) * gain_row.astype(F32)


def shift(value, axis, by):
    pairs = []
    for i in range(SIDE * SIDE):
        y, x = divmod(i, SIDE)
        if axis == "x":
            x = (x + by) % SIDE
        else:
            y = (y + by) % SIDE
        pairs.append((i, y * SIDE + x))
    return lax.ppermute(value, "mp", pairs)


def ring(value, axis):
    half = value.shape[0] // 2
    left = shift(value, axis, 1)
    right = shift(value, axis, -1)
    far = jnp.concatenate([shift(left[:half], axis, 1), shift(right[half:], axis, -1)], axis=0)
    return [value, left, right, far]


def twice(k):
    return ((k << 1) ^ ((k >> 3) * 19)) & 15


def halved(k):
    return (k >> 1) ^ ((k & 1) * 9)


def over_z(value):
    return lax.ppermute(value, "dp", [(0, 2), (1, 3), (2, 0), (3, 1)])


def dp_blocks(value, across):
    mate = [(0, 1), (1, 0), (2, 3), (3, 2)]
    return [value, lax.ppermute(value, "dp", mate), across, lax.ppermute(across, "dp", mate)]


def norm_kernel(value_ref, gain_ref, out_ref):
    out_ref[...] = layer_norm(value_ref[...], gain_ref[...]).astype(BF16)


def norm_rows(value, gain):
    return pl.pallas_call(
        norm_kernel, out_shape=jax.ShapeDtypeStruct(value.shape, BF16)
    )(value, gain)


def latent_kernel(piece_ref, weight_ref, base_ref, gain_ref, out_ref):
    width = RESAMPLE_HEAD_DIM
    share = piece_ref.shape[1] // width
    heads = weight_ref.shape[0] // width
    owned = piece_ref.shape[0] // heads
    piece = piece_ref[...].astype(F32)
    total = base_ref[...]
    for h in range(heads):
        rows = piece[h * owned : (h + 1) * owned]
        left = jnp.concatenate(
            [rows[:, j * width : (j + 1) * width] for j in range(share)], axis=0
        )
        total = total + jnp.dot(
            left.astype(BF16),
            weight_ref[h * width : (h + 1) * width, :],
            preferred_element_type=F32,
        )
    out_ref[...] = layer_norm(total, gain_ref[...]).astype(BF16)


def latent_rows(piece, weight, base, gain):
    return pl.pallas_call(
        latent_kernel,
        out_shape=jax.ShapeDtypeStruct(base.shape, BF16),
        compiler_params=pltpu.CompilerParams(vmem_limit_bytes=VMEM_LIMIT),
    )(piece, weight, base, gain)


def query_kernel(where, text_ref, *rest):
    weights = rest[:8]
    out_ref, held, centered, scale_ref, sems = rest[8:]
    rows, depth = text_ref.shape
    group, width = 64, 256
    parts = len(weights)
    block = weights[0].shape[0]
    copies = [pltpu.make_async_copy(w, held.at[j], sems.at[j]) for j, w in enumerate(weights)]
    first = pl.program_id(0) == 0

    @pl.when(first)
    def _():
        for copy in copies:
            copy.start()

    @pl.loop(0, rows // group)
    def _(step):
        at = pl.ds(pl.multiple_of(step * group, group), group)
        total = jnp.zeros((group, width), F32)
        for c in range(depth // width):
            total += text_ref[at, c * width : (c + 1) * width].astype(F32)
        mean = jnp.sum(total, axis=1, keepdims=True) * (1.0 / depth)
        square = jnp.zeros((group, width), F32)
        for c in range(depth // width):
            cols = slice(c * width, (c + 1) * width)
            off = text_ref[at, cols].astype(F32) - mean
            centered[at, cols] = off.astype(BF16)
            square += off * off
        spread = jnp.sum(square, axis=1, keepdims=True) * (1.0 / depth)
        scale_ref[at, :] = jnp.broadcast_to(lax.rsqrt(spread + 1e-05), (group, 128))

    @pl.when(first)
    def _():
        for copy in copies:
            copy.wait()

    total = None
    for j in range(parts):
        at = (where[j // 2] * 2 + j % 2) * block
        cols = pl.ds(pl.multiple_of(at, block), block)
        term = jnp.dot(centered[:, cols], held[j], preferred_element_type=F32)
        total = term if total is None else total + term
    out_ref[...] = (total * scale_ref[:, :1]).astype(BF16)


def query_matmul(text, weights, where):
    tokens, depth = text.shape
    cols = weights[0].shape[1]
    rows = 256
    return pl.pallas_call(
        query_kernel,
        grid_spec=pltpu.PrefetchScalarGridSpec(
            num_scalar_prefetch=1,
            grid=(tokens // rows,),
            in_specs=[pl.BlockSpec((rows, depth), lambda i, w: (i, 0))]
            + [pl.BlockSpec(memory_space=pl.ANY) for w in weights],
            out_specs=pl.BlockSpec((rows, cols), lambda i, w: (i, 0)),
            scratch_shapes=[
                pltpu.VMEM((len(weights),) + weights[0].shape, BF16),
                pltpu.VMEM((rows, depth), BF16),
                pltpu.VMEM((rows, 128), F32),
                pltpu.SemaphoreType.DMA((len(weights),)),
            ],
        ),
        out_shape=jax.ShapeDtypeStruct((tokens, cols), BF16),
        compiler_params=pltpu.CompilerParams(vmem_limit_bytes=VMEM_LIMIT),
    )(where, text, *weights)


def attend_kernel(
    count, order, where, gate_ref, q_ref, cot_ref, dest_ref, kv0, kv1, kv2, kv3,
    ctx_ref, part_ref, full, pairs, grads, acc, sems,
):
    tokens = q_ref.shape[0]
    keys = dest_ref.shape[0]
    block = kv0.shape[0]
    rows = 768
    gate = gate_ref[0]
    head = pl.program_id(0)
    heads = pl.num_programs(0)
    cols_k = pl.ds(pl.multiple_of(head * HD, HD), HD)
    cols_v = pl.ds(pl.multiple_of((head + heads) * HD, HD), HD)
    across = (((1,), (1,)), ((), ()))
    down = (((0,), (0,)), ((), ()))

    @pl.when(head == 0)
    def _():
        copies = []
        for j, weight in enumerate((kv0, kv1, kv2, kv3)):
            place = pl.ds(pl.multiple_of(where[j] * block, block), block)
            copies.append(pltpu.make_async_copy(weight, full.at[place, :], sems.at[j]))
        for copy in copies:
            copy.start()
        for copy in copies:
            copy.wait()
        pairs[...] = jnp.dot(dest_ref[...], full[...], preferred_element_type=F32).astype(BF16)

    key = pairs[:, cols_k]
    value = pairs[:, cols_v]
    slot = lax.broadcasted_iota(jnp.int32, (keys, 1), 0) % FMAX
    bias = jnp.where(slot < count[0], 0.0, -1e30)
    scale = 1.0 / math.sqrt(HD)
    for step in range(tokens // rows):
        at = slice(step * rows, (step + 1) * rows)
        q = q_ref[at, :]
        score = lax.dot_general(key, q, across, preferred_element_type=F32) + bias
        top = jnp.max(score, axis=0, keepdims=True)
        weight = jnp.exp((score - top) * scale)
        prob = weight * (1.0 / jnp.sum(weight, axis=0, keepdims=True))
        rounded = prob.astype(BF16)
        blend = lax.dot_general(value, rounded, down, preferred_element_type=F32)
        ctx_ref[at, :] = (gate * blend.T).astype(BF16)
        cot = (gate * cot_ref[at, :].astype(F32)).astype(BF16)
        d_prob = lax.dot_general(value, cot, across, preferred_element_type=F32)
        d_sum = jnp.sum(prob * d_prob, axis=0, keepdims=True)
        d_score = ((d_prob - d_sum) * prob).astype(BF16)
        grad_k = jnp.dot(d_score, q, preferred_element_type=F32)
        grad_v = jnp.dot(rounded, cot, preferred_element_type=F32)
        if step == 0:
            acc[:, :HD] = grad_k
            acc[:, HD:] = grad_v
        else:
            acc[:, :HD] += grad_k
            acc[:, HD:] += grad_v
    chunks = order.shape[0]
    size = keys // chunks
    for j in range(chunks):
        to = pl.ds(pl.multiple_of(order[j] * size, size), size)
        at = slice(j * size, (j + 1) * size)
        grads[to, cols_k] = (acc[at, :HD] * scale).astype(BF16)
        grads[to, cols_v] = acc[at, HD:].astype(BF16)

    @pl.when(head == heads - 1)
    def _():
        part_ref[...] = lax.dot_general(
            grads[...], full[...], across, preferred_element_type=F32
        ).astype(BF16)


def attention(query, dest, kv_blocks, cot, count, order, where, gate):
    tokens, cols = query.shape
    keys, width = dest.shape
    heads = cols // HD
    head = pl.BlockSpec((tokens, HD), lambda h, *_: (0, h))
    whole = lambda a: pl.BlockSpec(a.shape, lambda h, *_: (0, 0), pipeline_mode=pl.Buffered(1))
    return pl.pallas_call(
        attend_kernel,
        grid_spec=pltpu.PrefetchScalarGridSpec(
            num_scalar_prefetch=3,
            grid=(heads,),
            in_specs=[pl.BlockSpec(memory_space=pltpu.SMEM), head, head, whole(dest)]
            + [pl.BlockSpec(memory_space=pl.ANY) for w in kv_blocks],
            out_specs=[head, pl.BlockSpec((keys, width), lambda h, *_: (0, 0))],
            scratch_shapes=[
                pltpu.VMEM((width, 2 * cols), BF16),
                pltpu.VMEM((keys, 2 * cols), BF16),
                pltpu.VMEM((keys, 2 * cols), BF16),
                pltpu.VMEM((keys, 2 * HD), F32),
                pltpu.SemaphoreType.DMA((len(kv_blocks),)),
            ],
        ),
        out_shape=[
            jax.ShapeDtypeStruct((tokens, cols), BF16),
            jax.ShapeDtypeStruct((keys, width), BF16),
        ],
        compiler_params=pltpu.CompilerParams(vmem_limit_bytes=56 * 1024 * 1024),
    )(count, order, where, gate, query, cot, dest, *kv_blocks)


def per_device(
    frames,
    latent_init,
    norm_gains,
    res_query,
    res_kv,
    res_out,
    text,
    text_gain,
    w_query,
    w_kv,
    xgate,
    frame_counts,
    frame_dest,
    cotangent,
):
    mp_count = lax.axis_size("mp")
    group = lax.axis_index(GROUP)
    dp = lax.axis_index("dp")
    share = LAT // mp_count
    slots = frame_dest.shape[0]
    owned = frames.shape[0]
    groups = slots // owned
    width = res_query.shape[1]
    res_scale = 1.0 / math.sqrt(RESAMPLE_HEAD_DIM)

    whole_text = lax.all_gather(text[0, 0], "mp", axis=1, tiled=True)
    media = norm_rows(frames.reshape(-1, E), norm_gains[:1]).reshape(frames.shape)
    half = owned // 2
    ring_x = [ring(media[:half], "x"), ring(media[half:], "y")]
    kv_local = jnp.concatenate([w_kv[0, :, 0], w_kv[0, :, 1]], axis=1)
    kv_across = over_z(kv_local)
    depth = w_query.shape[1] // 2
    gain = lax.dynamic_slice_in_dim(text_gain[0], dp * 2 * depth, 2 * depth, 0)
    scaled = (w_query[0].astype(F32) * gain.astype(F32)[:, None]).astype(BF16)
    low_across = over_z(scaled[:depth])

    lat_norm = layer_norm(latent_init, norm_gains[1]).astype(BF16)
    res_pair = jnp.concatenate([res_kv[:, 0], res_kv[:, 1]], axis=1)
    res_q = jnp.dot(lat_norm, res_query, preferred_element_type=F32).astype(BF16)
    lat_pairs = jnp.dot(lat_norm, res_pair, preferred_element_type=F32).astype(BF16)
    media_halves = []
    joined_halves = [jnp.concatenate(blocks, axis=1) for blocks in ring_x]
    joined_halves, kv_across = lax.optimization_barrier((joined_halves, kv_across))
    for joined, axis in zip(joined_halves, ("y", "x")):
        parts = [
            jnp.einsum("fpe,ec->fpc", block, res_pair, preferred_element_type=F32).astype(BF16)
            for block in ring(joined, axis)
        ]
        media_halves.append(jnp.concatenate(parts, axis=1))
    media_halves, low_across = lax.optimization_barrier((media_halves, low_across))
    media_pairs = jnp.concatenate(media_halves, axis=0)
    pair_list = jnp.concatenate(
        [jnp.broadcast_to(lat_pairs, (owned,) + lat_pairs.shape), media_pairs], axis=1
    )
    score = (
        jnp.einsum("ld,fpd->flp", res_q, pair_list[:, :, :width], preferred_element_type=F32)
        * res_scale
    )
    weights = jnp.exp(score - jnp.max(score, axis=-1, keepdims=True))
    blend = jnp.einsum(
        "flp,fpd->fld", weights.astype(BF16), pair_list[:, :, width:], preferred_element_type=F32
    )
    res_context = (blend / jnp.sum(weights, axis=-1)[:, :, None]).astype(BF16)

    piece = res_context.reshape(owned, groups, share * width).swapaxes(0, 1)
    piece = lax.all_to_all(piece, GROUP, 0, 0, tiled=True).reshape(slots, share * width)
    piece, query_rest = lax.optimization_barrier((piece, scaled[depth:]))
    query_high = dp_blocks(query_rest, over_z(query_rest))
    query_low = dp_blocks(scaled[:depth], low_across)
    kv_blocks = dp_blocks(kv_local, kv_across)
    slot_ids = jnp.arange(slots, dtype=jnp.int32)
    target = (twice(group) ^ (slot_ids // owned)) * owned + slot_ids % owned
    to_dest = (frame_dest[None, :] == target[:, None]).astype(BF16)
    piece = jnp.dot(to_dest, piece, preferred_element_type=F32).astype(BF16)
    piece = lax.all_to_all(
        piece.reshape(mp_count, owned, share * width), "mp", 0, 0, tiled=True
    )
    base_rows = lax.dynamic_slice_in_dim(latent_init, group * share, share, 0).astype(F32)
    latents = latent_rows(
        piece.reshape(slots, share * width),
        res_out,
        jnp.repeat(base_rows, owned, axis=0),
        norm_gains[2:],
    )
    dp_count = lax.axis_size("dp")

    def place(g, m):
        return (g // dp_count * mp_count + m) * dp_count + g % dp_count

    mine = lax.ppermute(
        latents,
        ("segment", "mp", "dp"),
        [(place(g, m), place(twice(g) ^ m, m)) for g in range(groups) for m in range(mp_count)],
    )
    dest = lax.all_to_all(
        jnp.broadcast_to(mine, (mp_count,) + mine.shape), "mp", 0, 0, tiled=True
    ).reshape(LAT * owned, E)
    order = halved(group ^ jnp.arange(mp_count, dtype=jnp.int32))

    where = jnp.stack([dp, dp ^ 1, dp ^ 2, dp ^ 3]).astype(jnp.int32)
    query_blocks = [w for both in zip(query_low, query_high) for w in both]
    query = query_matmul(whole_text, query_blocks, where)
    dest, query = lax.optimization_barrier((dest, query))
    context, part = attention(
        query, dest, kv_blocks, cotangent[0, 0], frame_counts[0], order, where, jnp.tanh(xgate)
    )

    part = lax.all_to_all(part.reshape(mp_count, share * owned, E), "mp", 0, 0, tiled=True)
    dest_grad = jnp.sum(part.astype(F32), axis=0).astype(BF16)
    cut = groups // share
    send = (
        dest_grad.reshape(share, owned, cut, E // cut)
        .transpose(0, 2, 1, 3)
        .reshape(groups, owned, E // cut)
    )
    send = lax.all_to_all(send, GROUP, 0, 0, tiled=True).reshape(slots, E // cut)
    to_owner = (frame_dest[:, None] == slot_ids[None, :]).astype(BF16)
    send = jnp.dot(to_owner, send, preferred_element_type=F32).astype(BF16)
    send = lax.all_to_all(send.reshape(groups, owned, E // cut), GROUP, 0, 0, tiled=True)
    latent_grad = (
        send.reshape(share, cut, owned, E // cut)
        .transpose(0, 2, 1, 3)
        .reshape(share, owned, E)
        .astype(F32)
    )
    return (context[None, None], latent_grad)


def solution(mesh):
    in_specs = (
        P(("segment", "dp"), "mp", None),
        P(),
        P(),
        P(None, "mp"),
        P(None, None, "mp"),
        P(),
        P("segment", "dp", None, "mp"),
        P("segment", None),
        P("segment", "dp", "mp"),
        P("segment", "dp", None, "mp"),
        P("segment"),
        P("segment", "dp"),
        P(),
        P("segment", "dp", None, "mp"),
    )
    out_specs = (P("segment", "dp", None, "mp"), P("mp", ("segment", "dp"), None))
    return jax.shard_map(
        per_device, mesh=mesh, in_specs=in_specs, out_specs=out_specs, check_vma=False
    )
```

```python
import functools
import math

import jax
import jax.numpy as jnp
from jax import lax
from jax.experimental import pallas as pl
from jax.experimental.pallas import tpu as pltpu
from jax.sharding import PartitionSpec as P

HD = 128
E = 1536
RESAMPLE_HEAD_DIM = 96
PAD = 128
LAT = 64
FMAX = 8
SIDE = 4
GROUP = ("segment", "dp")
BF16 = jnp.bfloat16
F32 = jnp.float32
VMEM_LIMIT = 36 * 1024 * 1024


def layer_norm(inputs, gain_row):
    values = inputs.astype(F32)
    center = values - jnp.mean(values, axis=-1, keepdims=True)
    spread = jnp.mean(center * center, axis=-1, keepdims=True)
    return center * lax.rsqrt(spread + 1e-05) * gain_row.astype(F32)


def shift(value, axis, by):
    pairs = []
    for i in range(SIDE * SIDE):
        y, x = divmod(i, SIDE)
        if axis == "x":
            x = (x + by) % SIDE
        else:
            y = (y + by) % SIDE
        pairs.append((i, y * SIDE + x))
    return lax.ppermute(value, "mp", pairs)


def ring(value, axis):
    half = value.shape[0] // 2
    left = shift(value, axis, 1)
    right = shift(value, axis, -1)
    far = jnp.concatenate([shift(left[:half], axis, 1), shift(right[half:], axis, -1)], axis=0)
    return [value, left, right, far]


def direct(value, axis):
    return [value, shift(value, axis, 1), shift(value, axis, -1), shift(value, axis, 2)]


def twice(k):
    return ((k << 1) ^ ((k >> 3) * 19)) & 15


def halved(k):
    return (k >> 1) ^ ((k & 1) * 9)


def over_z(value):
    return lax.ppermute(value, "dp", [(0, 2), (1, 3), (2, 0), (3, 1)])


def dp_blocks(value, across):
    mate = [(0, 1), (1, 0), (2, 3), (3, 2)]
    return [value, lax.ppermute(value, "dp", mate), across, lax.ppermute(across, "dp", mate)]


def norm_kernel(value_ref, gain_ref, out_ref):
    out_ref[...] = layer_norm(value_ref[...], gain_ref[...]).astype(BF16)


def norm_rows(value, gain):
    return pl.pallas_call(
        norm_kernel, out_shape=jax.ShapeDtypeStruct(value.shape, BF16)
    )(value, gain)


def resample_kernel(q_ref, lat_ref, *rest):
    pieces, out_ref, held = rest[:-2], rest[-2], rest[-1]
    frames_each = pieces[0].shape[0]
    count = len(pieces) // 4 * frames_each
    q = q_ref[...]
    scale = 1.0 / math.sqrt(RESAMPLE_HEAD_DIM)
    groups = out_ref.shape[0] // count
    share = q.shape[0] // groups
    for f in range(count):
        first = f // frames_each * 4
        blocks = [pieces[first + j][f % frames_each] for j in range(4)]
        pair = jnp.concatenate([lat_ref[...]] + blocks, axis=0)
        score = scale * lax.dot_general(
            q, pair[:, :PAD], (((1,), (1,)), ((), ())), preferred_element_type=F32
        )
        weight = jnp.exp(score - jnp.max(score, axis=1, keepdims=True))
        blend = jnp.dot(weight.astype(BF16), pair[:, PAD:], preferred_element_type=F32)
        blend = blend / jnp.sum(weight, axis=1, keepdims=True)
        for j in range(share):
            to = pl.ds(j * groups * count + f, groups, stride=count)
            held[to, :] = blend[j * groups : (j + 1) * groups]
    for j in range(share):
        rows = slice(j * groups * count, (j + 1) * groups * count)
        out_ref[:, j * PAD : (j + 1) * PAD] = held[rows, :].astype(BF16)


def resample(q, lat_pairs, pieces, slots, share):
    return pl.pallas_call(
        resample_kernel,
        out_shape=jax.ShapeDtypeStruct((slots, share * PAD), BF16),
        scratch_shapes=[pltpu.VMEM((slots * share, PAD), F32)],
    )(q, lat_pairs, *pieces)


def latent_kernel(piece_ref, weight_ref, base_ref, gain_ref, out_ref):
    width = RESAMPLE_HEAD_DIM
    share = piece_ref.shape[1] // PAD
    heads = weight_ref.shape[0] // width
    owned = piece_ref.shape[0] // heads
    piece = piece_ref[...].astype(F32)
    total = base_ref[...]
    for h in range(heads):
        rows = piece[h * owned : (h + 1) * owned]
        left = jnp.concatenate([rows[:, j * PAD : (j + 1) * PAD] for j in range(share)], axis=0)
        total = total + jnp.dot(
            left[:, :width].astype(BF16),
            weight_ref[h * width : (h + 1) * width, :],
            preferred_element_type=F32,
        )
    out_ref[...] = layer_norm(total, gain_ref[...]).astype(BF16)


def latent_rows(piece, weight, base, gain):
    return pl.pallas_call(
        latent_kernel,
        out_shape=jax.ShapeDtypeStruct(base.shape, BF16),
        compiler_params=pltpu.CompilerParams(vmem_limit_bytes=56 * 1024 * 1024),
    )(piece, weight, base, gain)


def query_kernel(where, text_ref, *rest):
    weights = rest[:8]
    out_ref, held, centered, scale_ref, sems = rest[8:]
    rows, depth = text_ref.shape
    group, width = 64, 256
    block = depth // 4
    copies = []
    for j, weight in enumerate(weights):
        size = weight.shape[0]
        at = where[j // 2] * block + (j % 2) * (block - size)
        to = held.at[pl.ds(pl.multiple_of(at, 256), size), :]
        copies.append(pltpu.make_async_copy(weight, to, sems.at[j]))
    first = pl.program_id(0) == 0

    @pl.when(first)
    def _():
        for copy in copies:
            copy.start()

    @pl.loop(0, rows // group)
    def _(step):
        at = pl.ds(pl.multiple_of(step * group, group), group)
        total = jnp.zeros((group, width), F32)
        for c in range(depth // width):
            total += text_ref[at, c * width : (c + 1) * width].astype(F32)
        mean = jnp.sum(total, axis=1, keepdims=True) * (1.0 / depth)
        square = jnp.zeros((group, width), F32)
        for c in range(depth // width):
            cols = slice(c * width, (c + 1) * width)
            off = text_ref[at, cols].astype(F32) - mean
            centered[at, cols] = off.astype(BF16)
            square += off * off
        spread = jnp.sum(square, axis=1, keepdims=True) * (1.0 / depth)
        scale_ref[at, :] = jnp.broadcast_to(lax.rsqrt(spread + 1e-05), (group, 128))

    @pl.when(first)
    def _():
        for copy in copies:
            copy.wait()

    total = jnp.dot(centered[...], held[...], preferred_element_type=F32)
    out_ref[...] = (total * scale_ref[:, :1]).astype(BF16)


def query_matmul(text, weights, where):
    tokens, depth = text.shape
    cols = weights[0].shape[1]
    rows = 256
    return pl.pallas_call(
        query_kernel,
        grid_spec=pltpu.PrefetchScalarGridSpec(
            num_scalar_prefetch=1,
            grid=(tokens // rows,),
            in_specs=[pl.BlockSpec((rows, depth), lambda i, w: (i, 0))]
            + [pl.BlockSpec(memory_space=pl.ANY) for w in weights],
            out_specs=pl.BlockSpec((rows, cols), lambda i, w: (i, 0)),
            scratch_shapes=[
                pltpu.VMEM((depth, cols), BF16),
                pltpu.VMEM((rows, depth), BF16),
                pltpu.VMEM((rows, 128), F32),
                pltpu.SemaphoreType.DMA((len(weights),)),
            ],
        ),
        out_shape=jax.ShapeDtypeStruct((tokens, cols), BF16),
        compiler_params=pltpu.CompilerParams(vmem_limit_bytes=VMEM_LIMIT),
    )(where, text, *weights)


def attend_kernel(
    count, order, where, gate_ref, q_ref, cot_ref, dest_ref, kv0, kv1, kv2, kv3,
    ctx_ref, part_ref, full, pairs, grads, acc, sems,
):
    tokens = q_ref.shape[0]
    keys = dest_ref.shape[0]
    block = kv0.shape[0]
    rows = 768
    gate = gate_ref[0]
    head = pl.program_id(0)
    heads = pl.num_programs(0)
    cols_k = pl.ds(pl.multiple_of(head * HD, HD), HD)
    cols_v = pl.ds(pl.multiple_of((head + heads) * HD, HD), HD)
    across = (((1,), (1,)), ((), ()))
    down = (((0,), (0,)), ((), ()))

    @pl.when(head == 0)
    def _():
        copies = []
        for j, weight in enumerate((kv0, kv1, kv2, kv3)):
            place = pl.ds(pl.multiple_of(where[j] * block, block), block)
            copies.append(pltpu.make_async_copy(weight, full.at[place, :], sems.at[j]))
        for copy in copies:
            copy.start()
        for copy in copies:
            copy.wait()
        pairs[...] = jnp.dot(dest_ref[...], full[...], preferred_element_type=F32).astype(BF16)

    key = pairs[:, cols_k]
    value = pairs[:, cols_v]
    slot = lax.broadcasted_iota(jnp.int32, (keys, 1), 0) % FMAX
    bias = jnp.where(slot < count[0], 0.0, -1e30)
    scale = 1.0 / math.sqrt(HD)
    for step in range(tokens // rows):
        at = slice(step * rows, (step + 1) * rows)
        q = q_ref[at, :]
        score = lax.dot_general(key, q, across, preferred_element_type=F32) + bias
        top = jnp.max(score, axis=0, keepdims=True)
        weight = jnp.exp((score - top) * scale)
        prob = weight * (1.0 / jnp.sum(weight, axis=0, keepdims=True))
        rounded = prob.astype(BF16)
        blend = lax.dot_general(value, rounded, down, preferred_element_type=F32)
        ctx_ref[at, :] = (gate * blend.T).astype(BF16)
        cot = (gate * cot_ref[at, :].astype(F32)).astype(BF16)
        d_prob = lax.dot_general(value, cot, across, preferred_element_type=F32)
        d_sum = jnp.sum(prob * d_prob, axis=0, keepdims=True)
        d_score = ((d_prob - d_sum) * prob).astype(BF16)
        grad_k = jnp.dot(d_score, q, preferred_element_type=F32)
        grad_v = jnp.dot(rounded, cot, preferred_element_type=F32)
        if step == 0:
            acc[:, :HD] = grad_k
            acc[:, HD:] = grad_v
        else:
            acc[:, :HD] += grad_k
            acc[:, HD:] += grad_v
    chunks = order.shape[0]
    size = keys // chunks
    for j in range(chunks):
        to = pl.ds(pl.multiple_of(order[j] * size, size), size)
        at = slice(j * size, (j + 1) * size)
        grads[to, cols_k] = (acc[at, :HD] * scale).astype(BF16)
        grads[to, cols_v] = acc[at, HD:].astype(BF16)

    @pl.when(head == heads - 1)
    def _():
        part_ref[...] = lax.dot_general(
            grads[...], full[...], across, preferred_element_type=F32
        ).astype(BF16)


def attention(query, dest, kv_blocks, cot, count, order, where, gate):
    tokens, cols = query.shape
    keys, width = dest.shape
    heads = cols // HD
    head = pl.BlockSpec((tokens, HD), lambda h, *_: (0, h))
    whole = lambda a: pl.BlockSpec(a.shape, lambda h, *_: (0, 0), pipeline_mode=pl.Buffered(1))
    return pl.pallas_call(
        attend_kernel,
        grid_spec=pltpu.PrefetchScalarGridSpec(
            num_scalar_prefetch=3,
            grid=(heads,),
            in_specs=[pl.BlockSpec(memory_space=pltpu.SMEM), head, head, whole(dest)]
            + [pl.BlockSpec(memory_space=pl.ANY) for w in kv_blocks],
            out_specs=[head, pl.BlockSpec((keys, width), lambda h, *_: (0, 0))],
            scratch_shapes=[
                pltpu.VMEM((width, 2 * cols), BF16),
                pltpu.VMEM((keys, 2 * cols), BF16),
                pltpu.VMEM((keys, 2 * cols), BF16),
                pltpu.VMEM((keys, 2 * HD), F32),
                pltpu.SemaphoreType.DMA((len(kv_blocks),)),
            ],
        ),
        out_shape=[
            jax.ShapeDtypeStruct((tokens, cols), BF16),
            jax.ShapeDtypeStruct((keys, width), BF16),
        ],
        compiler_params=pltpu.CompilerParams(vmem_limit_bytes=56 * 1024 * 1024),
    )(count, order, where, gate, query, cot, dest, *kv_blocks)


def per_device(
    frames,
    latent_init,
    norm_gains,
    res_query,
    res_kv,
    res_out,
    text,
    text_gain,
    w_query,
    w_kv,
    xgate,
    frame_counts,
    frame_dest,
    cotangent,
):
    mp_count = lax.axis_size("mp")
    group = lax.axis_index(GROUP)
    dp = lax.axis_index("dp")
    share = LAT // mp_count
    slots = frame_dest.shape[0]
    owned = frames.shape[0]
    groups = slots // owned
    width = res_query.shape[1]

    whole_text = lax.all_gather(text[0, 0], "mp", axis=1, tiled=True)
    media = norm_rows(frames.reshape(-1, E), norm_gains[:1]).reshape(frames.shape)
    half = owned // 2
    phase = [direct(media[:half], "x"), direct(media[half:], "y")]
    joined_halves = [jnp.concatenate(blocks, axis=1) for blocks in phase]
    joined_halves, w_kv, w_query = lax.optimization_barrier((joined_halves, w_kv, w_query))
    kv_local = jnp.concatenate([w_kv[0, :, 0], w_kv[0, :, 1]], axis=1)
    kv_across = over_z(kv_local)
    depth = w_query.shape[1]
    early = depth * 3 // 8
    gain = lax.dynamic_slice_in_dim(text_gain[0], dp * depth, depth, 0)
    scaled = (w_query[0].astype(F32) * gain.astype(F32)[:, None]).astype(BF16)
    low_across = over_z(scaled[:early])

    lat_rows = latent_init.reshape(groups, share, E).swapaxes(0, 1).reshape(LAT, E)
    lat_norm = layer_norm(lat_rows, norm_gains[1]).astype(BF16)
    pad = lambda a: jnp.pad(a, ((0, 0), (0, PAD - width)))
    res_pair = jnp.concatenate([pad(res_kv[:, 0]), pad(res_kv[:, 1])], axis=1)
    res_q = jnp.dot(lat_norm, pad(res_query), preferred_element_type=F32).astype(BF16)
    lat_pairs = jnp.dot(lat_norm, res_pair, preferred_element_type=F32).astype(BF16)
    pieces = []
    for joined, axis in zip(joined_halves, ("y", "x")):
        for block in ring(joined, axis):
            pieces.append(
                jnp.einsum("fpe,ec->fpc", block, res_pair, preferred_element_type=F32).astype(BF16)
            )
    pieces, low_across, kv_across = lax.optimization_barrier((pieces, low_across, kv_across))
    piece = resample(res_q, lat_pairs, pieces, slots, share)

    piece = lax.all_to_all(
        piece.reshape(groups, owned, share * PAD), GROUP, 0, 0, tiled=True
    ).reshape(slots, share * PAD)
    piece, query_rest = lax.optimization_barrier((piece, scaled[early:]))
    high_across = over_z(query_rest)
    slot_ids = jnp.arange(slots, dtype=jnp.int32)
    target = (twice(group) ^ (slot_ids // owned)) * owned + slot_ids % owned
    to_dest = (frame_dest[None, :] == target[:, None]).astype(BF16)
    piece = jnp.dot(to_dest, piece, preferred_element_type=F32).astype(BF16)
    piece = lax.all_to_all(
        piece.reshape(mp_count, owned, share * PAD), "mp", 0, 0, tiled=True
    )
    base_rows = lax.dynamic_slice_in_dim(latent_init, group * share, share, 0).astype(F32)
    latents = latent_rows(
        piece.reshape(slots, share * PAD),
        res_out,
        jnp.repeat(base_rows, owned, axis=0),
        norm_gains[2:],
    )
    dp_count = lax.axis_size("dp")

    def place(g, m):
        return (g // dp_count * mp_count + m) * dp_count + g % dp_count

    mine = lax.ppermute(
        latents,
        ("segment", "mp", "dp"),
        [(place(g, m), place(twice(g) ^ m, m)) for g in range(groups) for m in range(mp_count)],
    )
    crossed = (high_across, low_across, kv_across)
    high_across, low_across, kv_across = lax.optimization_barrier((crossed, mine))[0]
    query_high = dp_blocks(query_rest, high_across)
    query_low = dp_blocks(scaled[:early], low_across)
    kv_blocks = dp_blocks(kv_local, kv_across)
    dest = lax.all_to_all(
        jnp.broadcast_to(mine, (mp_count,) + mine.shape), "mp", 0, 0, tiled=True
    ).reshape(LAT * owned, E)
    order = halved(group ^ jnp.arange(mp_count, dtype=jnp.int32))

    where = jnp.stack([dp, dp ^ 1, dp ^ 2, dp ^ 3]).astype(jnp.int32)
    query_blocks = [w for both in zip(query_low, query_high) for w in both]
    query = query_matmul(whole_text, query_blocks, where)
    dest, query = lax.optimization_barrier((dest, query))
    context, part = attention(
        query, dest, kv_blocks, cotangent[0, 0], frame_counts[0], order, where, jnp.tanh(xgate)
    )

    part = lax.all_to_all(part.reshape(mp_count, share * owned, E), "mp", 0, 0, tiled=True)
    dest_grad = jnp.sum(part.astype(F32), axis=0).astype(BF16)
    cut = groups // share
    send = (
        dest_grad.reshape(share, owned, cut, E // cut)
        .transpose(0, 2, 1, 3)
        .reshape(groups, owned, E // cut)
    )
    send = lax.all_to_all(send, GROUP, 0, 0, tiled=True).reshape(slots, E // cut)
    to_owner = (frame_dest[:, None] == slot_ids[None, :]).astype(BF16)
    send = jnp.dot(to_owner, send, preferred_element_type=F32).astype(BF16)
    send = lax.all_to_all(send.reshape(groups, owned, E // cut), GROUP, 0, 0, tiled=True)
    latent_grad = (
        send.reshape(share, cut, owned, E // cut)
        .transpose(0, 2, 1, 3)
        .reshape(share, owned, E)
        .astype(F32)
    )
    return (context[None, None], latent_grad)


def solution(mesh):
    in_specs = (
        P(("segment", "dp"), "mp", None),
        P(),
        P(),
        P(None, "mp"),
        P(None, None, "mp"),
        P(),
        P("segment", "dp", None, "mp"),
        P("segment", None),
        P("segment", "dp", "mp"),
        P("segment", "dp", None, "mp"),
        P("segment"),
        P("segment", "dp"),
        P(),
        P("segment", "dp", None, "mp"),
    )
    out_specs = (P("segment", "dp", None, "mp"), P("mp", ("segment", "dp"), None))
    return jax.shard_map(
        per_device, mesh=mesh, in_specs=in_specs, out_specs=out_specs, check_vma=False
    )
```

```python
import functools
import math

import jax
import jax.numpy as jnp
from jax import lax
from jax.experimental import pallas as pl
from jax.experimental.pallas import tpu as pltpu
from jax.sharding import PartitionSpec as P

HD = 128
E = 1536
RESAMPLE_HEAD_DIM = 96
PAD = 128
LAT = 64
FMAX = 8
SIDE = 4
GROUP = ("segment", "dp")
BF16 = jnp.bfloat16
F32 = jnp.float32
VMEM_LIMIT = 36 * 1024 * 1024


def layer_norm(inputs, gain_row):
    values = inputs.astype(F32)
    center = values - jnp.mean(values, axis=-1, keepdims=True)
    spread = jnp.mean(center * center, axis=-1, keepdims=True)
    return center * lax.rsqrt(spread + 1e-05) * gain_row.astype(F32)


def shift(value, axis, by):
    pairs = []
    for i in range(SIDE * SIDE):
        y, x = divmod(i, SIDE)
        if axis == "x":
            x = (x + by) % SIDE
        else:
            y = (y + by) % SIDE
        pairs.append((i, y * SIDE + x))
    return lax.ppermute(value, "mp", pairs)


def ring(value, axis):
    half = value.shape[0] // 2
    left = shift(value, axis, 1)
    right = shift(value, axis, -1)
    far = jnp.concatenate([shift(left[:half], axis, 1), shift(right[half:], axis, -1)], axis=0)
    return [value, left, right, far]


def direct(value, axis):
    return [value, shift(value, axis, 1), shift(value, axis, -1), shift(value, axis, 2)]


def twice(k):
    return ((k << 1) ^ ((k >> 3) * 19)) & 15


def halved(k):
    return (k >> 1) ^ ((k & 1) * 9)


def over_z(value):
    return lax.ppermute(value, "dp", [(0, 2), (1, 3), (2, 0), (3, 1)])


def core_swap(value):
    return lax.ppermute(value, "dp", [(0, 1), (1, 0), (2, 3), (3, 2)])


def dp_blocks(value, across):
    return [value, core_swap(value), across, core_swap(across)]


def norm_kernel(value_ref, gain_ref, out_ref):
    out_ref[...] = layer_norm(value_ref[...], gain_ref[...]).astype(BF16)


def norm_rows(value, gain):
    return pl.pallas_call(
        norm_kernel, out_shape=jax.ShapeDtypeStruct(value.shape, BF16)
    )(value, gain)


def resample_kernel(q_ref, lat_ref, *rest):
    pieces, out_ref, held = rest[:-2], rest[-2], rest[-1]
    frames_each = pieces[0].shape[0]
    count = len(pieces) // 4 * frames_each
    q = q_ref[...]
    scale = 1.0 / math.sqrt(RESAMPLE_HEAD_DIM)
    groups = out_ref.shape[0] // count
    share = q.shape[0] // groups
    for f in range(count):
        first = f // frames_each * 4
        blocks = [pieces[first + j][f % frames_each] for j in range(4)]
        pair = jnp.concatenate([lat_ref[...]] + blocks, axis=0)
        score = scale * lax.dot_general(
            q, pair[:, :PAD], (((1,), (1,)), ((), ())), preferred_element_type=F32
        )
        weight = jnp.exp(score - jnp.max(score, axis=1, keepdims=True))
        blend = jnp.dot(weight.astype(BF16), pair[:, PAD:], preferred_element_type=F32)
        blend = blend / jnp.sum(weight, axis=1, keepdims=True)
        for j in range(share):
            to = pl.ds(j * groups * count + f, groups, stride=count)
            held[to, :] = blend[j * groups : (j + 1) * groups]
    for j in range(share):
        rows = slice(j * groups * count, (j + 1) * groups * count)
        out_ref[:, j * PAD : (j + 1) * PAD] = held[rows, :].astype(BF16)


def resample(q, lat_pairs, pieces, slots, share):
    return pl.pallas_call(
        resample_kernel,
        out_shape=jax.ShapeDtypeStruct((slots, share * PAD), BF16),
        scratch_shapes=[pltpu.VMEM((slots * share, PAD), F32)],
    )(q, lat_pairs, *pieces)


def latent_kernel(piece_ref, weight_ref, base_ref, gain_ref, out_ref):
    width = RESAMPLE_HEAD_DIM
    share = piece_ref.shape[1] // PAD
    heads = weight_ref.shape[0] // width
    owned = piece_ref.shape[0] // heads
    piece = piece_ref[...].astype(F32)
    total = base_ref[...]
    for h in range(heads):
        rows = piece[h * owned : (h + 1) * owned]
        left = jnp.concatenate([rows[:, j * PAD : (j + 1) * PAD] for j in range(share)], axis=0)
        total = total + jnp.dot(
            left[:, :width].astype(BF16),
            weight_ref[h * width : (h + 1) * width, :],
            preferred_element_type=F32,
        )
    out_ref[...] = layer_norm(total, gain_ref[...]).astype(BF16)


def latent_rows(piece, weight, base, gain):
    return pl.pallas_call(
        latent_kernel,
        out_shape=jax.ShapeDtypeStruct(base.shape, BF16),
        compiler_params=pltpu.CompilerParams(vmem_limit_bytes=56 * 1024 * 1024),
    )(piece, weight, base, gain)


def query_kernel(where, text_ref, gain_ref, *rest):
    weights = rest[:-5]
    out_ref, held, centered, scale_ref, sems = rest[-5:]
    rows, depth = text_ref.shape
    group, width = 64, 256
    block = depth // 4
    copies = []
    filled = 0
    for j, weight in enumerate(weights):
        size = weight.shape[0]
        at = where[filled // block] * block + filled % block
        filled += size
        to = held.at[pl.ds(pl.multiple_of(at, 512), size), :]
        copies.append(pltpu.make_async_copy(weight, to, sems.at[j]))
    first = pl.program_id(0) == 0

    @pl.when(first)
    def _():
        for copy in copies:
            copy.start()

    @pl.loop(0, rows // group)
    def _(step):
        at = pl.ds(pl.multiple_of(step * group, group), group)
        total = jnp.zeros((group, width), F32)
        for c in range(depth // width):
            total += text_ref[at, c * width : (c + 1) * width].astype(F32)
        mean = jnp.sum(total, axis=1, keepdims=True) * (1.0 / depth)
        square = jnp.zeros((group, width), F32)
        for c in range(depth // width):
            cols = slice(c * width, (c + 1) * width)
            off = text_ref[at, cols].astype(F32) - mean
            centered[at, cols] = (off * gain_ref[:, cols].astype(F32)).astype(BF16)
            square += off * off
        spread = jnp.sum(square, axis=1, keepdims=True) * (1.0 / depth)
        scale_ref[at, :] = jnp.broadcast_to(lax.rsqrt(spread + 1e-05), (group, 128))

    @pl.when(first)
    def _():
        for copy in copies:
            copy.wait()

    total = jnp.dot(centered[...], held[...], preferred_element_type=F32)
    out_ref[...] = (total * scale_ref[:, :1]).astype(BF16)


def query_matmul(text, gain, weights, where):
    tokens, depth = text.shape
    cols = weights[0].shape[1]
    rows = 256
    return pl.pallas_call(
        query_kernel,
        grid_spec=pltpu.PrefetchScalarGridSpec(
            num_scalar_prefetch=1,
            grid=(tokens // rows,),
            in_specs=[
                pl.BlockSpec((rows, depth), lambda i, w: (i, 0)),
                pl.BlockSpec((1, depth), lambda i, w: (0, 0)),
            ]
            + [pl.BlockSpec(memory_space=pl.ANY) for w in weights],
            out_specs=pl.BlockSpec((rows, cols), lambda i, w: (i, 0)),
            scratch_shapes=[
                pltpu.VMEM((depth, cols), BF16),
                pltpu.VMEM((rows, depth), BF16),
                pltpu.VMEM((rows, 128), F32),
                pltpu.SemaphoreType.DMA((len(weights),)),
            ],
        ),
        out_shape=jax.ShapeDtypeStruct((tokens, cols), BF16),
        compiler_params=pltpu.CompilerParams(vmem_limit_bytes=VMEM_LIMIT),
    )(where, text, gain, *weights)


def attend_kernel(
    count, order, where, gate_ref, q_ref, cot_ref, dest_ref, kv0, kv1, kv2, kv3,
    ctx_ref, part_ref, full, pairs, grads, acc, sems,
):
    tokens = q_ref.shape[0]
    keys = dest_ref.shape[0]
    block = kv0.shape[0]
    rows = 768
    gate = gate_ref[0]
    head = pl.program_id(0)
    heads = pl.num_programs(0)
    cols_k = pl.ds(pl.multiple_of(head * HD, HD), HD)
    cols_v = pl.ds(pl.multiple_of((head + heads) * HD, HD), HD)
    across = (((1,), (1,)), ((), ()))
    down = (((0,), (0,)), ((), ()))

    @pl.when(head == 0)
    def _():
        copies = []
        for j, weight in enumerate((kv0, kv1, kv2, kv3)):
            place = pl.ds(pl.multiple_of(where[j] * block, block), block)
            copies.append(pltpu.make_async_copy(weight, full.at[place, :], sems.at[j]))
        for copy in copies:
            copy.start()
        for copy in copies:
            copy.wait()
        pairs[...] = jnp.dot(dest_ref[...], full[...], preferred_element_type=F32).astype(BF16)

    key = pairs[:, cols_k]
    value = pairs[:, cols_v]
    slot = lax.broadcasted_iota(jnp.int32, (keys, 1), 0) % FMAX
    bias = jnp.where(slot < count[0], 0.0, -1e30)
    scale = 1.0 / math.sqrt(HD)
    for step in range(tokens // rows):
        at = slice(step * rows, (step + 1) * rows)
        q = q_ref[at, :]
        score = lax.dot_general(key, q, across, preferred_element_type=F32) + bias
        top = jnp.max(score, axis=0, keepdims=True)
        weight = jnp.exp((score - top) * scale)
        prob = weight * (1.0 / jnp.sum(weight, axis=0, keepdims=True))
        rounded = prob.astype(BF16)
        blend = lax.dot_general(value, rounded, down, preferred_element_type=F32)
        ctx_ref[at, :] = (gate * blend.T).astype(BF16)
        cot = (gate * cot_ref[at, :].astype(F32)).astype(BF16)
        d_prob = lax.dot_general(value, cot, across, preferred_element_type=F32)
        d_sum = jnp.sum(prob * d_prob, axis=0, keepdims=True)
        d_score = ((d_prob - d_sum) * prob).astype(BF16)
        grad_k = jnp.dot(d_score, q, preferred_element_type=F32)
        grad_v = jnp.dot(rounded, cot, preferred_element_type=F32)
        if step == 0:
            acc[:, :HD] = grad_k
            acc[:, HD:] = grad_v
        else:
            acc[:, :HD] += grad_k
            acc[:, HD:] += grad_v
    chunks = order.shape[0]
    size = keys // chunks
    for j in range(chunks):
        to = pl.ds(pl.multiple_of(order[j] * size, size), size)
        at = slice(j * size, (j + 1) * size)
        grads[to, cols_k] = (acc[at, :HD] * scale).astype(BF16)
        grads[to, cols_v] = acc[at, HD:].astype(BF16)

    @pl.when(head == heads - 1)
    def _():
        part_ref[...] = lax.dot_general(
            grads[...], full[...], across, preferred_element_type=F32
        ).astype(BF16)


def attention(query, dest, kv_blocks, cot, count, order, where, gate):
    tokens, cols = query.shape
    keys, width = dest.shape
    heads = cols // HD
    head = pl.BlockSpec((tokens, HD), lambda h, *_: (0, h))
    whole = lambda a: pl.BlockSpec(a.shape, lambda h, *_: (0, 0), pipeline_mode=pl.Buffered(1))
    return pl.pallas_call(
        attend_kernel,
        grid_spec=pltpu.PrefetchScalarGridSpec(
            num_scalar_prefetch=3,
            grid=(heads,),
            in_specs=[pl.BlockSpec(memory_space=pltpu.SMEM), head, head, whole(dest)]
            + [pl.BlockSpec(memory_space=pl.ANY) for w in kv_blocks],
            out_specs=[head, pl.BlockSpec((keys, width), lambda h, *_: (0, 0))],
            scratch_shapes=[
                pltpu.VMEM((width, 2 * cols), BF16),
                pltpu.VMEM((keys, 2 * cols), BF16),
                pltpu.VMEM((keys, 2 * cols), BF16),
                pltpu.VMEM((keys, 2 * HD), F32),
                pltpu.SemaphoreType.DMA((len(kv_blocks),)),
            ],
        ),
        out_shape=[
            jax.ShapeDtypeStruct((tokens, cols), BF16),
            jax.ShapeDtypeStruct((keys, width), BF16),
        ],
        compiler_params=pltpu.CompilerParams(vmem_limit_bytes=56 * 1024 * 1024),
    )(count, order, where, gate, query, cot, dest, *kv_blocks)


def per_device(
    frames,
    latent_init,
    norm_gains,
    res_query,
    res_kv,
    res_out,
    text,
    text_gain,
    w_query,
    w_kv,
    xgate,
    frame_counts,
    frame_dest,
    cotangent,
):
    mp_count = lax.axis_size("mp")
    group = lax.axis_index(GROUP)
    dp = lax.axis_index("dp")
    share = LAT // mp_count
    slots = frame_dest.shape[0]
    owned = frames.shape[0]
    groups = slots // owned
    width = res_query.shape[1]

    whole_text = lax.all_gather(text[0, 0], "mp", axis=1, tiled=True)
    media = norm_rows(frames.reshape(-1, E), norm_gains[:1]).reshape(frames.shape)
    half = owned // 2
    phase = [direct(media[:half], "x"), direct(media[half:], "y")]
    joined_halves = [jnp.concatenate(blocks, axis=1) for blocks in phase]
    early = w_query.shape[1] // 4
    low_across = over_z(w_query[0, :early])
    high_across = over_z(w_query[0, early:])
    joined_halves, low_across = lax.optimization_barrier((joined_halves, low_across))
    joined_halves, w_kv = lax.optimization_barrier((joined_halves, w_kv))
    kv_local = jnp.concatenate([w_kv[0, :, 0], w_kv[0, :, 1]], axis=1)

    lat_rows = latent_init.reshape(groups, share, E).swapaxes(0, 1).reshape(LAT, E)
    lat_norm = layer_norm(lat_rows, norm_gains[1]).astype(BF16)
    pad = lambda a: jnp.pad(a, ((0, 0), (0, PAD - width)))
    res_pair = jnp.concatenate([pad(res_kv[:, 0]), pad(res_kv[:, 1])], axis=1)
    res_q = jnp.dot(lat_norm, pad(res_query), preferred_element_type=F32).astype(BF16)
    lat_pairs = jnp.dot(lat_norm, res_pair, preferred_element_type=F32).astype(BF16)
    pieces = []
    for joined, axis in zip(joined_halves, ("y", "x")):
        for block in ring(joined, axis):
            pieces.append(
                jnp.einsum("fpe,ec->fpc", block, res_pair, preferred_element_type=F32).astype(BF16)
            )
    pieces, high_across, kv_local = lax.optimization_barrier((pieces, high_across, kv_local))
    piece = resample(res_q, lat_pairs, pieces, slots, share)

    piece = lax.all_to_all(
        piece.reshape(groups, owned, share * PAD), GROUP, 0, 0, tiled=True
    ).reshape(slots, share * PAD)
    crossed = (low_across, high_across)
    piece, crossed, kv_local = lax.optimization_barrier((piece, crossed, kv_local))
    query_blocks = [w_query[0], core_swap(w_query[0]), *crossed]
    query_blocks += [core_swap(w) for w in crossed]
    kv_across = over_z(kv_local)
    slot_ids = jnp.arange(slots, dtype=jnp.int32)
    target = (twice(group) ^ (slot_ids // owned)) * owned + slot_ids % owned
    to_dest = (frame_dest[None, :] == target[:, None]).astype(BF16)
    piece = jnp.dot(to_dest, piece, preferred_element_type=F32).astype(BF16)
    piece = lax.all_to_all(
        piece.reshape(mp_count, owned, share * PAD), "mp", 0, 0, tiled=True
    )
    base_rows = lax.dynamic_slice_in_dim(latent_init, group * share, share, 0).astype(F32)
    latents = latent_rows(
        piece.reshape(slots, share * PAD),
        res_out,
        jnp.repeat(base_rows, owned, axis=0),
        norm_gains[2:],
    )
    latents, kv_across = lax.optimization_barrier((latents, kv_across))
    dp_count = lax.axis_size("dp")

    def place(g, m):
        return (g // dp_count * mp_count + m) * dp_count + g % dp_count

    mine = lax.ppermute(
        latents,
        ("segment", "mp", "dp"),
        [(place(g, m), place(twice(g) ^ m, m)) for g in range(groups) for m in range(mp_count)],
    )
    kv_across = lax.optimization_barrier((kv_across, mine))[0]
    kv_blocks = dp_blocks(kv_local, kv_across)
    dest = lax.all_to_all(
        jnp.broadcast_to(mine, (mp_count,) + mine.shape), "mp", 0, 0, tiled=True
    ).reshape(LAT * owned, E)
    order = halved(group ^ jnp.arange(mp_count, dtype=jnp.int32))

    where = jnp.stack([dp, dp ^ 1, dp ^ 2, dp ^ 3]).astype(jnp.int32)
    query = query_matmul(whole_text, text_gain, query_blocks, where)
    dest, query = lax.optimization_barrier((dest, query))
    context, part = attention(
        query, dest, kv_blocks, cotangent[0, 0], frame_counts[0], order, where, jnp.tanh(xgate)
    )

    part = lax.all_to_all(part.reshape(mp_count, share * owned, E), "mp", 0, 0, tiled=True)
    dest_grad = jnp.sum(part.astype(F32), axis=0).astype(BF16)
    cut = groups // share
    send = (
        dest_grad.reshape(share, owned, cut, E // cut)
        .transpose(0, 2, 1, 3)
        .reshape(groups, owned, E // cut)
    )
    send = lax.all_to_all(send, GROUP, 0, 0, tiled=True).reshape(slots, E // cut)
    to_owner = (frame_dest[:, None] == slot_ids[None, :]).astype(BF16)
    send = jnp.dot(to_owner, send, preferred_element_type=F32).astype(BF16)
    send = lax.all_to_all(send.reshape(groups, owned, E // cut), GROUP, 0, 0, tiled=True)
    latent_grad = (
        send.reshape(share, cut, owned, E // cut)
        .transpose(0, 2, 1, 3)
        .reshape(share, owned, E)
        .astype(F32)
    )
    return (context[None, None], latent_grad)


def solution(mesh):
    in_specs = (
        P(("segment", "dp"), "mp", None),
        P(),
        P(),
        P(None, "mp"),
        P(None, None, "mp"),
        P(),
        P("segment", "dp", None, "mp"),
        P("segment", None),
        P("segment", "dp", "mp"),
        P("segment", "dp", None, "mp"),
        P("segment"),
        P("segment", "dp"),
        P(),
        P("segment", "dp", None, "mp"),
    )
    out_specs = (P("segment", "dp", None, "mp"), P("mp", ("segment", "dp"), None))
    return jax.shard_map(
        per_device, mesh=mesh, in_specs=in_specs, out_specs=out_specs, check_vma=False
    )
```

```python
import functools
import math

import jax
import jax.numpy as jnp
from jax import lax
from jax.experimental import pallas as pl
from jax.experimental.pallas import tpu as pltpu
from jax.sharding import PartitionSpec as P

HD = 128
E = 1536
RESAMPLE_HEAD_DIM = 96
PAD = 128
LAT = 64
FMAX = 8
SIDE = 4
GROUP = ("segment", "dp")
BF16 = jnp.bfloat16
F32 = jnp.float32
VMEM_LIMIT = 36 * 1024 * 1024


def layer_norm(inputs, gain_row):
    values = inputs.astype(F32)
    center = values - jnp.mean(values, axis=-1, keepdims=True)
    spread = jnp.mean(center * center, axis=-1, keepdims=True)
    return center * lax.rsqrt(spread + 1e-05) * gain_row.astype(F32)


def shift(value, axis, by):
    pairs = []
    for i in range(SIDE * SIDE):
        y, x = divmod(i, SIDE)
        if axis == "x":
            x = (x + by) % SIDE
        else:
            y = (y + by) % SIDE
        pairs.append((i, y * SIDE + x))
    return lax.ppermute(value, "mp", pairs)


def ring(value, axis):
    half = value.shape[0] // 2
    left = shift(value, axis, 1)
    right = shift(value, axis, -1)
    far = jnp.concatenate([shift(left[:half], axis, 1), shift(right[half:], axis, -1)], axis=0)
    return [value, left, right, far]


def direct(value, axis):
    return [value, shift(value, axis, 1), shift(value, axis, -1), shift(value, axis, 2)]


def twice(k):
    return ((k << 1) ^ ((k >> 3) * 19)) & 15


def halved(k):
    return (k >> 1) ^ ((k & 1) * 9)


def over_z(value):
    return lax.ppermute(value, "dp", [(0, 2), (1, 3), (2, 0), (3, 1)])


def core_swap(value):
    return lax.ppermute(value, "dp", [(0, 1), (1, 0), (2, 3), (3, 2)])


def dp_blocks(value, across):
    return [value, core_swap(value), across, core_swap(across)]


def norm_kernel(value_ref, gains_ref, low_ref, high_ref):
    gain = gains_ref[...].astype(F32)[:1]
    half = low_ref.shape[0]
    low_ref[...] = layer_norm(value_ref[:half, :], gain).astype(BF16)
    high_ref[...] = layer_norm(value_ref[half:, :], gain).astype(BF16)


def norm_halves(value, gains):
    half = jax.ShapeDtypeStruct((value.shape[0] // 2, value.shape[1]), BF16)
    return pl.pallas_call(norm_kernel, out_shape=[half, half])(value, gains)


def resample_kernel(q_ref, lat_ref, *rest):
    pieces, out_ref, held = rest[:-2], rest[-2], rest[-1]
    frames_each = pieces[0].shape[0]
    count = len(pieces) // 4 * frames_each
    q = q_ref[...]
    scale = 1.0 / math.sqrt(RESAMPLE_HEAD_DIM)
    groups = out_ref.shape[0] // count
    share = q.shape[0] // groups
    for f in range(count):
        first = f // frames_each * 4
        blocks = [pieces[first + j][f % frames_each] for j in range(4)]
        pair = jnp.concatenate([lat_ref[...]] + blocks, axis=0)
        score = scale * lax.dot_general(
            q, pair[:, :PAD], (((1,), (1,)), ((), ())), preferred_element_type=F32
        )
        weight = jnp.exp(score - jnp.max(score, axis=1, keepdims=True))
        blend = jnp.dot(weight.astype(BF16), pair[:, PAD:], preferred_element_type=F32)
        blend = blend / jnp.sum(weight, axis=1, keepdims=True)
        for j in range(share):
            to = pl.ds(j * groups * count + f, groups, stride=count)
            held[to, :] = blend[j * groups : (j + 1) * groups]
    for j in range(share):
        rows = slice(j * groups * count, (j + 1) * groups * count)
        out_ref[:, j * PAD : (j + 1) * PAD] = held[rows, :].astype(BF16)


def resample(q, lat_pairs, pieces, slots, share):
    return pl.pallas_call(
        resample_kernel,
        out_shape=jax.ShapeDtypeStruct((slots, share * PAD), BF16),
        scratch_shapes=[pltpu.VMEM((slots * share, PAD), F32)],
    )(q, lat_pairs, *pieces)


def latent_kernel(piece_ref, weight_ref, base_ref, gain_ref, out_ref):
    width = RESAMPLE_HEAD_DIM
    share = piece_ref.shape[1] // PAD
    heads = weight_ref.shape[0] // width
    owned = piece_ref.shape[0] // heads
    piece = piece_ref[...].astype(F32)
    total = base_ref[...]
    for h in range(heads):
        rows = piece[h * owned : (h + 1) * owned]
        left = jnp.concatenate([rows[:, j * PAD : (j + 1) * PAD] for j in range(share)], axis=0)
        total = total + jnp.dot(
            left[:, :width].astype(BF16),
            weight_ref[h * width : (h + 1) * width, :],
            preferred_element_type=F32,
        )
    out_ref[...] = layer_norm(total, gain_ref[...]).astype(BF16)


def latent_rows(piece, weight, base, gain):
    return pl.pallas_call(
        latent_kernel,
        out_shape=jax.ShapeDtypeStruct(base.shape, BF16),
        compiler_params=pltpu.CompilerParams(vmem_limit_bytes=56 * 1024 * 1024),
    )(piece, weight, base, gain)


def query_kernel(where, text_ref, gain_ref, *rest):
    weights = rest[:-5]
    out_ref, held, centered, scale_ref, sems = rest[-5:]
    rows, depth = text_ref.shape
    group, width = 64, 256
    block = depth // 4
    copies = []
    filled = 0
    for j, weight in enumerate(weights):
        size = weight.shape[0]
        at = where[filled // block] * block + filled % block
        filled += size
        to = held.at[pl.ds(pl.multiple_of(at, 512), size), :]
        copies.append(pltpu.make_async_copy(weight, to, sems.at[j]))
    first = pl.program_id(0) == 0

    @pl.when(first)
    def _():
        for copy in copies:
            copy.start()

    @pl.loop(0, rows // group)
    def _(step):
        at = pl.ds(pl.multiple_of(step * group, group), group)
        total = jnp.zeros((group, width), F32)
        for c in range(depth // width):
            total += text_ref[at, c * width : (c + 1) * width].astype(F32)
        mean = jnp.sum(total, axis=1, keepdims=True) * (1.0 / depth)
        square = jnp.zeros((group, width), F32)
        for c in range(depth // width):
            cols = slice(c * width, (c + 1) * width)
            off = text_ref[at, cols].astype(F32) - mean
            centered[at, cols] = (off * gain_ref[:, cols].astype(F32)).astype(BF16)
            square += off * off
        spread = jnp.sum(square, axis=1, keepdims=True) * (1.0 / depth)
        scale_ref[at, :] = jnp.broadcast_to(lax.rsqrt(spread + 1e-05), (group, 128))

    @pl.when(first)
    def _():
        for copy in copies:
            copy.wait()

    total = jnp.dot(centered[...], held[...], preferred_element_type=F32)
    out_ref[...] = (total * scale_ref[:, :1]).astype(BF16)


def query_matmul(text, gain, weights, where):
    tokens, depth = text.shape
    cols = weights[0].shape[1]
    rows = 256
    return pl.pallas_call(
        query_kernel,
        grid_spec=pltpu.PrefetchScalarGridSpec(
            num_scalar_prefetch=1,
            grid=(tokens // rows,),
            in_specs=[
                pl.BlockSpec((rows, depth), lambda i, w: (i, 0)),
                pl.BlockSpec((1, depth), lambda i, w: (0, 0)),
            ]
            + [pl.BlockSpec(memory_space=pl.ANY) for w in weights],
            out_specs=pl.BlockSpec((rows, cols), lambda i, w: (i, 0)),
            scratch_shapes=[
                pltpu.VMEM((depth, cols), BF16),
                pltpu.VMEM((rows, depth), BF16),
                pltpu.VMEM((rows, 128), F32),
                pltpu.SemaphoreType.DMA((len(weights),)),
            ],
        ),
        out_shape=jax.ShapeDtypeStruct((tokens, cols), BF16),
        compiler_params=pltpu.CompilerParams(vmem_limit_bytes=VMEM_LIMIT),
    )(where, text, gain, *weights)


def attend_kernel(
    count, order, where, gate_ref, q_ref, cot_ref, dest_ref, kv0, kv1, kv2, kv3,
    ctx_ref, part_ref, full, pairs, grads, acc, sems,
):
    tokens = q_ref.shape[0]
    keys = dest_ref.shape[0]
    block = kv0.shape[0]
    rows = 768
    gate = gate_ref[0]
    head = pl.program_id(0)
    heads = pl.num_programs(0)
    cols_k = pl.ds(pl.multiple_of(head * HD, HD), HD)
    cols_v = pl.ds(pl.multiple_of((head + heads) * HD, HD), HD)
    across = (((1,), (1,)), ((), ()))
    down = (((0,), (0,)), ((), ()))

    @pl.when(head == 0)
    def _():
        copies = []
        for j, weight in enumerate((kv0, kv1, kv2, kv3)):
            place = pl.ds(pl.multiple_of(where[j] * block, block), block)
            copies.append(pltpu.make_async_copy(weight, full.at[place, :], sems.at[j]))
        for copy in copies:
            copy.start()
        for copy in copies:
            copy.wait()
        pairs[...] = jnp.dot(dest_ref[...], full[...], preferred_element_type=F32).astype(BF16)

    key = pairs[:, cols_k]
    value = pairs[:, cols_v]
    slot = lax.broadcasted_iota(jnp.int32, (keys, 1), 0) % FMAX
    bias = jnp.where(slot < count[0], 0.0, -1e30)
    scale = 1.0 / math.sqrt(HD)
    for step in range(tokens // rows):
        at = slice(step * rows, (step + 1) * rows)
        q = q_ref[at, :]
        score = lax.dot_general(key, q, across, preferred_element_type=F32) + bias
        top = jnp.max(score, axis=0, keepdims=True)
        weight = jnp.exp((score - top) * scale)
        prob = weight * (1.0 / jnp.sum(weight, axis=0, keepdims=True))
        rounded = prob.astype(BF16)
        blend = lax.dot_general(value, rounded, down, preferred_element_type=F32)
        ctx_ref[at, :] = (gate * blend.T).astype(BF16)
        cot = (gate * cot_ref[at, :].astype(F32)).astype(BF16)
        d_prob = lax.dot_general(value, cot, across, preferred_element_type=F32)
        d_sum = jnp.sum(prob * d_prob, axis=0, keepdims=True)
        d_score = ((d_prob - d_sum) * prob).astype(BF16)
        grad_k = jnp.dot(d_score, q, preferred_element_type=F32)
        grad_v = jnp.dot(rounded, cot, preferred_element_type=F32)
        if step == 0:
            acc[:, :HD] = grad_k
            acc[:, HD:] = grad_v
        else:
            acc[:, :HD] += grad_k
            acc[:, HD:] += grad_v
    chunks = order.shape[0]
    size = keys // chunks
    for j in range(chunks):
        to = pl.ds(pl.multiple_of(order[j] * size, size), size)
        at = slice(j * size, (j + 1) * size)
        grads[to, cols_k] = (acc[at, :HD] * scale).astype(BF16)
        grads[to, cols_v] = acc[at, HD:].astype(BF16)

    @pl.when(head == heads - 1)
    def _():
        part_ref[...] = lax.dot_general(
            grads[...], full[...], across, preferred_element_type=F32
        ).astype(BF16)


def attention(query, dest, kv_blocks, cot, count, order, where, gate):
    tokens, cols = query.shape
    keys, width = dest.shape
    heads = cols // HD
    head = pl.BlockSpec((tokens, HD), lambda h, *_: (0, h))
    whole = lambda a: pl.BlockSpec(a.shape, lambda h, *_: (0, 0), pipeline_mode=pl.Buffered(1))
    return pl.pallas_call(
        attend_kernel,
        grid_spec=pltpu.PrefetchScalarGridSpec(
            num_scalar_prefetch=3,
            grid=(heads,),
            in_specs=[pl.BlockSpec(memory_space=pltpu.SMEM), head, head, whole(dest)]
            + [pl.BlockSpec(memory_space=pl.ANY) for w in kv_blocks],
            out_specs=[head, pl.BlockSpec((keys, width), lambda h, *_: (0, 0))],
            scratch_shapes=[
                pltpu.VMEM((width, 2 * cols), BF16),
                pltpu.VMEM((keys, 2 * cols), BF16),
                pltpu.VMEM((keys, 2 * cols), BF16),
                pltpu.VMEM((keys, 2 * HD), F32),
                pltpu.SemaphoreType.DMA((len(kv_blocks),)),
            ],
        ),
        out_shape=[
            jax.ShapeDtypeStruct((tokens, cols), BF16),
            jax.ShapeDtypeStruct((keys, width), BF16),
        ],
        compiler_params=pltpu.CompilerParams(vmem_limit_bytes=56 * 1024 * 1024),
    )(count, order, where, gate, query, cot, dest, *kv_blocks)


def per_device(
    frames,
    latent_init,
    norm_gains,
    res_query,
    res_kv,
    res_out,
    text,
    text_gain,
    w_query,
    w_kv,
    xgate,
    frame_counts,
    frame_dest,
    cotangent,
):
    mp_count = lax.axis_size("mp")
    group = lax.axis_index(GROUP)
    dp = lax.axis_index("dp")
    share = LAT // mp_count
    slots = frame_dest.shape[0]
    owned = frames.shape[0]
    groups = slots // owned
    width = res_query.shape[1]

    whole_text = lax.all_gather(text[0, 0], "mp", axis=1, tiled=True)
    low, high = norm_halves(frames.reshape(-1, E), norm_gains)
    half_shape = (owned // 2,) + frames.shape[1:]
    phase = [direct(low.reshape(half_shape), "x"), direct(high.reshape(half_shape), "y")]
    joined_halves = [jnp.concatenate(blocks, axis=1) for blocks in phase]
    early = w_query.shape[1] // 4
    low_across = over_z(w_query[0, :early])
    high_across = over_z(w_query[0, early:])
    joined_halves, low_across = lax.optimization_barrier((joined_halves, low_across))
    joined_halves, w_kv = lax.optimization_barrier((joined_halves, w_kv))
    kv_local = jnp.concatenate([w_kv[0, :, 0], w_kv[0, :, 1]], axis=1)

    lat_rows = latent_init.reshape(groups, share, E).swapaxes(0, 1).reshape(LAT, E)
    lat_norm = layer_norm(lat_rows, norm_gains[1]).astype(BF16)
    pad = lambda a: jnp.pad(a, ((0, 0), (0, PAD - width)))
    res_pair = jnp.concatenate([pad(res_kv[:, 0]), pad(res_kv[:, 1])], axis=1)
    res_q = jnp.dot(lat_norm, pad(res_query), preferred_element_type=F32).astype(BF16)
    lat_pairs = jnp.dot(lat_norm, res_pair, preferred_element_type=F32).astype(BF16)
    pieces = []
    for joined, axis in zip(joined_halves, ("y", "x")):
        for block in ring(joined, axis):
            pieces.append(
                jnp.einsum("fpe,ec->fpc", block, res_pair, preferred_element_type=F32).astype(BF16)
            )
    order = halved(group ^ jnp.arange(mp_count, dtype=jnp.int32))
    where = jnp.stack([dp, dp ^ 1, dp ^ 2, dp ^ 3]).astype(jnp.int32)
    pieces, high_across, kv_local, order, where = lax.optimization_barrier(
        (pieces, high_across, kv_local, order, where)
    )
    piece = resample(res_q, lat_pairs, pieces, slots, share)

    piece = lax.all_to_all(
        piece.reshape(groups, owned, share * PAD), GROUP, 0, 0, tiled=True
    ).reshape(slots, share * PAD)
    crossed = (low_across, high_across)
    piece, crossed, kv_local = lax.optimization_barrier((piece, crossed, kv_local))
    query_blocks = [w_query[0], core_swap(w_query[0]), *crossed]
    query_blocks += [core_swap(w) for w in crossed]
    kv_across = over_z(kv_local)
    slot_ids = jnp.arange(slots, dtype=jnp.int32)
    target = (twice(group) ^ (slot_ids // owned)) * owned + slot_ids % owned
    to_dest = (frame_dest[None, :] == target[:, None]).astype(BF16)
    piece = jnp.dot(to_dest, piece, preferred_element_type=F32).astype(BF16)
    piece = lax.all_to_all(
        piece.reshape(mp_count, owned, share * PAD), "mp", 0, 0, tiled=True
    )
    base_rows = lax.dynamic_slice_in_dim(latent_init, group * share, share, 0).astype(F32)
    latents = latent_rows(
        piece.reshape(slots, share * PAD),
        res_out,
        jnp.repeat(base_rows, owned, axis=0),
        norm_gains[2:],
    )
    latents, kv_across = lax.optimization_barrier((latents, kv_across))
    dp_count = lax.axis_size("dp")

    def place(g, m):
        return (g // dp_count * mp_count + m) * dp_count + g % dp_count

    mine = lax.ppermute(
        latents,
        ("segment", "mp", "dp"),
        [(place(g, m), place(twice(g) ^ m, m)) for g in range(groups) for m in range(mp_count)],
    )
    kv_across = lax.optimization_barrier((kv_across, mine))[0]
    kv_blocks = dp_blocks(kv_local, kv_across)
    dest = lax.all_to_all(
        jnp.broadcast_to(mine, (mp_count,) + mine.shape), "mp", 0, 0, tiled=True
    ).reshape(LAT * owned, E)

    query = query_matmul(whole_text, text_gain, query_blocks, where)
    dest, query = lax.optimization_barrier((dest, query))
    context, part = attention(
        query, dest, kv_blocks, cotangent[0, 0], frame_counts[0], order, where, jnp.tanh(xgate)
    )

    part = lax.all_to_all(part.reshape(mp_count, share * owned, E), "mp", 0, 0, tiled=True)
    dest_grad = jnp.sum(part.astype(F32), axis=0).astype(BF16)
    cut = groups // share
    send = (
        dest_grad.reshape(share, owned, cut, E // cut)
        .transpose(0, 2, 1, 3)
        .reshape(groups, owned, E // cut)
    )
    send = lax.all_to_all(send, GROUP, 0, 0, tiled=True).reshape(slots, E // cut)
    to_owner = (frame_dest[:, None] == slot_ids[None, :]).astype(BF16)
    send = jnp.dot(to_owner, send, preferred_element_type=F32).astype(BF16)
    send = lax.all_to_all(send.reshape(groups, owned, E // cut), GROUP, 0, 0, tiled=True)
    latent_grad = (
        send.reshape(share, cut, owned, E // cut)
        .transpose(0, 2, 1, 3)
        .reshape(share, owned, E)
        .astype(F32)
    )
    return (context[None, None], latent_grad)


def solution(mesh):
    in_specs = (
        P(("segment", "dp"), "mp", None),
        P(),
        P(),
        P(None, "mp"),
        P(None, None, "mp"),
        P(),
        P("segment", "dp", None, "mp"),
        P("segment", None),
        P("segment", "dp", "mp"),
        P("segment", "dp", None, "mp"),
        P("segment"),
        P("segment", "dp"),
        P(),
        P("segment", "dp", None, "mp"),
    )
    out_specs = (P("segment", "dp", None, "mp"), P("mp", ("segment", "dp"), None))
    return jax.shard_map(
        per_device, mesh=mesh, in_specs=in_specs, out_specs=out_specs, check_vma=False
    )
```

```python
import functools
import math

import jax
import jax.numpy as jnp
from jax import lax
from jax.experimental import pallas as pl
from jax.experimental.pallas import tpu as pltpu
from jax.sharding import PartitionSpec as P

HD = 128
E = 1536
RESAMPLE_HEAD_DIM = 96
PAD = 128
LAT = 64
FMAX = 8
SIDE = 4
GROUP = ("segment", "dp")
BF16 = jnp.bfloat16
F32 = jnp.float32
VMEM_LIMIT = 36 * 1024 * 1024


def layer_norm(inputs, gain_row):
    values = inputs.astype(F32)
    center = values - jnp.mean(values, axis=-1, keepdims=True)
    spread = jnp.mean(center * center, axis=-1, keepdims=True)
    return center * lax.rsqrt(spread + 1e-05) * gain_row.astype(F32)


def shift(value, axis, by):
    pairs = []
    for i in range(SIDE * SIDE):
        y, x = divmod(i, SIDE)
        if axis == "x":
            x = (x + by) % SIDE
        else:
            y = (y + by) % SIDE
        pairs.append((i, y * SIDE + x))
    return lax.ppermute(value, "mp", pairs)


def ring(value, axis):
    half = value.shape[0] // 2
    left = shift(value, axis, 1)
    right = shift(value, axis, -1)
    far = jnp.concatenate([shift(left[:half], axis, 1), shift(right[half:], axis, -1)], axis=0)
    return [value, left, right, far]


def direct(value, axis):
    return [value, shift(value, axis, 1), shift(value, axis, -1), shift(value, axis, 2)]


def twice(k):
    return ((k << 1) ^ ((k >> 3) * 19)) & 15


def halved(k):
    return (k >> 1) ^ ((k & 1) * 9)


def over_z(value):
    return lax.ppermute(value, "dp", [(0, 2), (1, 3), (2, 0), (3, 1)])


def core_swap(value):
    return lax.ppermute(value, "dp", [(0, 1), (1, 0), (2, 3), (3, 2)])


def dp_blocks(value, across):
    return [value, core_swap(value), across, core_swap(across)]


def norm_kernel(value_ref, gains_ref, low_ref, high_ref):
    gain = gains_ref[...].astype(F32)[:1]
    half = low_ref.shape[0]
    low_ref[...] = layer_norm(value_ref[:half, :], gain).astype(BF16)
    high_ref[...] = layer_norm(value_ref[half:, :], gain).astype(BF16)


def norm_halves(value, gains):
    half = jax.ShapeDtypeStruct((value.shape[0] // 2, value.shape[1]), BF16)
    return pl.pallas_call(norm_kernel, out_shape=[half, half])(value, gains)


def resample_kernel(q_ref, lat_ref, *rest):
    pieces, out_ref, held = rest[:-2], rest[-2], rest[-1]
    frames_each = pieces[0].shape[0]
    count = len(pieces) // 4 * frames_each
    q = q_ref[...]
    scale = 1.0 / math.sqrt(RESAMPLE_HEAD_DIM)
    groups = out_ref.shape[0] // count
    share = q.shape[0] // groups
    for f in range(count):
        first = f // frames_each * 4
        blocks = [pieces[first + j][f % frames_each] for j in range(4)]
        pair = jnp.concatenate([lat_ref[...]] + blocks, axis=0)
        score = scale * lax.dot_general(
            q, pair[:, :PAD], (((1,), (1,)), ((), ())), preferred_element_type=F32
        )
        weight = jnp.exp(score - jnp.max(score, axis=1, keepdims=True))
        blend = jnp.dot(weight.astype(BF16), pair[:, PAD:], preferred_element_type=F32)
        blend = blend / jnp.sum(weight, axis=1, keepdims=True)
        for j in range(share):
            to = pl.ds(j * groups * count + f, groups, stride=count)
            held[to, :] = blend[j * groups : (j + 1) * groups]
    for j in range(share):
        rows = slice(j * groups * count, (j + 1) * groups * count)
        out_ref[:, j * PAD : (j + 1) * PAD] = held[rows, :].astype(BF16)


def resample(q, lat_pairs, pieces, slots, share):
    return pl.pallas_call(
        resample_kernel,
        out_shape=jax.ShapeDtypeStruct((slots, share * PAD), BF16),
        scratch_shapes=[pltpu.VMEM((slots * share, PAD), F32)],
    )(q, lat_pairs, *pieces)


def latent_kernel(piece_ref, weight_ref, base_ref, gain_ref, out_ref):
    width = RESAMPLE_HEAD_DIM
    share = piece_ref.shape[1] // PAD
    heads = weight_ref.shape[0] // width
    owned = piece_ref.shape[0] // heads
    piece = piece_ref[...].astype(F32)
    total = base_ref[...]
    for h in range(heads):
        rows = piece[h * owned : (h + 1) * owned]
        left = jnp.concatenate([rows[:, j * PAD : (j + 1) * PAD] for j in range(share)], axis=0)
        total = total + jnp.dot(
            left[:, :width].astype(BF16),
            weight_ref[h * width : (h + 1) * width, :],
            preferred_element_type=F32,
        )
    out_ref[...] = layer_norm(total, gain_ref[...]).astype(BF16)


def latent_rows(piece, weight, base, gain):
    return pl.pallas_call(
        latent_kernel,
        out_shape=jax.ShapeDtypeStruct(base.shape, BF16),
        compiler_params=pltpu.CompilerParams(vmem_limit_bytes=56 * 1024 * 1024),
    )(piece, weight, base, gain)


def query_kernel(where, text_ref, gain_ref, *rest):
    weights = rest[:-5]
    out_ref, held, centered, scale_ref, sems = rest[-5:]
    senders, rows, sent = text_ref.shape
    depth = senders * sent
    group, width = 64, 256
    block = depth // 4
    copies = []
    filled = 0
    for j, weight in enumerate(weights):
        size = weight.shape[0]
        at = where[filled // block] * block + filled % block
        filled += size
        to = held.at[pl.ds(pl.multiple_of(at, 512), size), :]
        copies.append(pltpu.make_async_copy(weight, to, sems.at[j]))
    first = pl.program_id(0) == 0
    each = sent // width

    def chunk(c):
        return c // each, slice(c % each * width, (c % each + 1) * width)

    @pl.when(first)
    def _():
        for copy in copies:
            copy.start()

    @pl.loop(0, rows // group)
    def _(step):
        at = pl.ds(pl.multiple_of(step * group, group), group)
        total = jnp.zeros((group, width), F32)
        for c in range(depth // width):
            total += text_ref[chunk(c)[0], at, chunk(c)[1]].astype(F32)
        mean = jnp.sum(total, axis=1, keepdims=True) * (1.0 / depth)
        square = jnp.zeros((group, width), F32)
        for c in range(depth // width):
            cols = slice(c * width, (c + 1) * width)
            off = text_ref[chunk(c)[0], at, chunk(c)[1]].astype(F32) - mean
            centered[at, cols] = (off * gain_ref[:, cols].astype(F32)).astype(BF16)
            square += off * off
        spread = jnp.sum(square, axis=1, keepdims=True) * (1.0 / depth)
        scale_ref[at, :] = jnp.broadcast_to(lax.rsqrt(spread + 1e-05), (group, 128))

    @pl.when(first)
    def _():
        for copy in copies:
            copy.wait()

    total = jnp.dot(centered[...], held[...], preferred_element_type=F32)
    out_ref[...] = (total * scale_ref[:, :1]).astype(BF16)


def query_matmul(text, gain, weights, where):
    senders, tokens, sent = text.shape
    depth = senders * sent
    cols = weights[0].shape[1]
    rows = 256
    return pl.pallas_call(
        query_kernel,
        grid_spec=pltpu.PrefetchScalarGridSpec(
            num_scalar_prefetch=1,
            grid=(tokens // rows,),
            in_specs=[
                pl.BlockSpec((senders, rows, sent), lambda i, w: (0, i, 0)),
                pl.BlockSpec((1, depth), lambda i, w: (0, 0)),
            ]
            + [pl.BlockSpec(memory_space=pl.ANY) for w in weights],
            out_specs=pl.BlockSpec((rows, cols), lambda i, w: (i, 0)),
            scratch_shapes=[
                pltpu.VMEM((depth, cols), BF16),
                pltpu.VMEM((rows, depth), BF16),
                pltpu.VMEM((rows, 128), F32),
                pltpu.SemaphoreType.DMA((len(weights),)),
            ],
        ),
        out_shape=jax.ShapeDtypeStruct((tokens, cols), BF16),
        compiler_params=pltpu.CompilerParams(vmem_limit_bytes=VMEM_LIMIT),
    )(where, text, gain, *weights)


def attend_kernel(
    count, order, where, gate_ref, q_ref, cot_ref, dest_ref, kv0, kv1, kv2, kv3,
    ctx_ref, part_ref, full, pairs, grads, acc, sems,
):
    tokens = q_ref.shape[0]
    keys = dest_ref.shape[0]
    block = kv0.shape[0]
    rows = 768
    gate = gate_ref[0]
    head = pl.program_id(0)
    heads = pl.num_programs(0)
    cols_k = pl.ds(pl.multiple_of(head * HD, HD), HD)
    cols_v = pl.ds(pl.multiple_of((head + heads) * HD, HD), HD)
    across = (((1,), (1,)), ((), ()))
    down = (((0,), (0,)), ((), ()))

    @pl.when(head == 0)
    def _():
        copies = []
        for j, weight in enumerate((kv0, kv1, kv2, kv3)):
            place = pl.ds(pl.multiple_of(where[j] * block, block), block)
            copies.append(pltpu.make_async_copy(weight, full.at[place, :], sems.at[j]))
        for copy in copies:
            copy.start()
        for copy in copies:
            copy.wait()
        pairs[...] = jnp.dot(dest_ref[...], full[...], preferred_element_type=F32).astype(BF16)

    key = pairs[:, cols_k]
    value = pairs[:, cols_v]
    slot = lax.broadcasted_iota(jnp.int32, (keys, 1), 0) % FMAX
    bias = jnp.where(slot < count[0], 0.0, -1e30)
    scale = 1.0 / math.sqrt(HD)
    for step in range(tokens // rows):
        at = slice(step * rows, (step + 1) * rows)
        q = q_ref[at, :]
        score = lax.dot_general(key, q, across, preferred_element_type=F32) + bias
        top = jnp.max(score, axis=0, keepdims=True)
        weight = jnp.exp((score - top) * scale)
        prob = weight * (1.0 / jnp.sum(weight, axis=0, keepdims=True))
        rounded = prob.astype(BF16)
        blend = lax.dot_general(value, rounded, down, preferred_element_type=F32)
        ctx_ref[at, :] = (gate * blend.T).astype(BF16)
        cot = (gate * cot_ref[at, :].astype(F32)).astype(BF16)
        d_prob = lax.dot_general(value, cot, across, preferred_element_type=F32)
        d_sum = jnp.sum(prob * d_prob, axis=0, keepdims=True)
        d_score = ((d_prob - d_sum) * prob).astype(BF16)
        grad_k = jnp.dot(d_score, q, preferred_element_type=F32)
        grad_v = jnp.dot(rounded, cot, preferred_element_type=F32)
        if step == 0:
            acc[:, :HD] = grad_k
            acc[:, HD:] = grad_v
        else:
            acc[:, :HD] += grad_k
            acc[:, HD:] += grad_v
    chunks = order.shape[0]
    size = keys // chunks
    for j in range(chunks):
        to = pl.ds(pl.multiple_of(order[j] * size, size), size)
        at = slice(j * size, (j + 1) * size)
        grads[to, cols_k] = (acc[at, :HD] * scale).astype(BF16)
        grads[to, cols_v] = acc[at, HD:].astype(BF16)

    @pl.when(head == heads - 1)
    def _():
        part_ref[...] = lax.dot_general(
            grads[...], full[...], across, preferred_element_type=F32
        ).astype(BF16)


def attention(query, dest, kv_blocks, cot, count, order, where, gate):
    tokens, cols = query.shape
    keys, width = dest.shape
    heads = cols // HD
    head = pl.BlockSpec((tokens, HD), lambda h, *_: (0, h))
    whole = lambda a: pl.BlockSpec(a.shape, lambda h, *_: (0, 0), pipeline_mode=pl.Buffered(1))
    return pl.pallas_call(
        attend_kernel,
        grid_spec=pltpu.PrefetchScalarGridSpec(
            num_scalar_prefetch=3,
            grid=(heads,),
            in_specs=[pl.BlockSpec(memory_space=pltpu.SMEM), head, head, whole(dest)]
            + [pl.BlockSpec(memory_space=pl.ANY) for w in kv_blocks],
            out_specs=[head, pl.BlockSpec((keys, width), lambda h, *_: (0, 0))],
            scratch_shapes=[
                pltpu.VMEM((width, 2 * cols), BF16),
                pltpu.VMEM((keys, 2 * cols), BF16),
                pltpu.VMEM((keys, 2 * cols), BF16),
                pltpu.VMEM((keys, 2 * HD), F32),
                pltpu.SemaphoreType.DMA((len(kv_blocks),)),
            ],
        ),
        out_shape=[
            jax.ShapeDtypeStruct((tokens, cols), BF16),
            jax.ShapeDtypeStruct((keys, width), BF16),
        ],
        compiler_params=pltpu.CompilerParams(vmem_limit_bytes=56 * 1024 * 1024),
    )(count, order, where, gate, query, cot, dest, *kv_blocks)


def per_device(
    frames,
    latent_init,
    norm_gains,
    res_query,
    res_kv,
    res_out,
    text,
    text_gain,
    w_query,
    w_kv,
    xgate,
    frame_counts,
    frame_dest,
    cotangent,
):
    mp_count = lax.axis_size("mp")
    group = lax.axis_index(GROUP)
    dp = lax.axis_index("dp")
    share = LAT // mp_count
    slots = frame_dest.shape[0]
    owned = frames.shape[0]
    groups = slots // owned
    width = res_query.shape[1]

    whole_text = lax.all_gather(text[0, 0], "mp", axis=0)
    low, high = norm_halves(frames.reshape(-1, E), norm_gains)
    half_shape = (owned // 2,) + frames.shape[1:]
    phase = [direct(low.reshape(half_shape), "x"), direct(high.reshape(half_shape), "y")]
    joined_halves = [jnp.concatenate(blocks, axis=1) for blocks in phase]
    early = w_query.shape[1] // 4
    low_across = over_z(w_query[0, :early])
    high_across = over_z(w_query[0, early:])
    joined_halves, low_across = lax.optimization_barrier((joined_halves, low_across))
    joined_halves, w_kv = lax.optimization_barrier((joined_halves, w_kv))
    kv_local = jnp.concatenate([w_kv[0, :, 0], w_kv[0, :, 1]], axis=1)

    lat_rows = latent_init.reshape(groups, share, E).swapaxes(0, 1).reshape(LAT, E)
    lat_norm = layer_norm(lat_rows, norm_gains[1]).astype(BF16)
    pad = lambda a: jnp.pad(a, ((0, 0), (0, PAD - width)))
    res_pair = jnp.concatenate([pad(res_kv[:, 0]), pad(res_kv[:, 1])], axis=1)
    res_q = jnp.dot(lat_norm, pad(res_query), preferred_element_type=F32).astype(BF16)
    lat_pairs = jnp.dot(lat_norm, res_pair, preferred_element_type=F32).astype(BF16)
    pieces = []
    for joined, axis in zip(joined_halves, ("y", "x")):
        for block in ring(joined, axis):
            pieces.append(
                jnp.einsum("fpe,ec->fpc", block, res_pair, preferred_element_type=F32).astype(BF16)
            )
    order = halved(group ^ jnp.arange(mp_count, dtype=jnp.int32))
    where = jnp.stack([dp, dp ^ 1, dp ^ 2, dp ^ 3]).astype(jnp.int32)
    pieces, high_across, kv_local, order, where = lax.optimization_barrier(
        (pieces, high_across, kv_local, order, where)
    )
    piece = resample(res_q, lat_pairs, pieces, slots, share)

    piece = lax.all_to_all(
        piece.reshape(groups, owned, share * PAD), GROUP, 0, 0, tiled=True
    ).reshape(slots, share * PAD)
    crossed = (low_across, high_across)
    piece, crossed, kv_local = lax.optimization_barrier((piece, crossed, kv_local))
    query_blocks = [w_query[0], core_swap(w_query[0]), *crossed]
    query_blocks += [core_swap(w) for w in crossed]
    kv_across = over_z(kv_local)
    slot_ids = jnp.arange(slots, dtype=jnp.int32)
    target = (twice(group) ^ (slot_ids // owned)) * owned + slot_ids % owned
    to_dest = (frame_dest[None, :] == target[:, None]).astype(BF16)
    piece = jnp.dot(to_dest, piece, preferred_element_type=F32).astype(BF16)
    piece = lax.all_to_all(
        piece.reshape(mp_count, owned, share * PAD), "mp", 0, 0, tiled=True
    )
    base_rows = lax.dynamic_slice_in_dim(latent_init, group * share, share, 0).astype(F32)
    latents = latent_rows(
        piece.reshape(slots, share * PAD),
        res_out,
        jnp.repeat(base_rows, owned, axis=0),
        norm_gains[2:],
    )
    latents, kv_across = lax.optimization_barrier((latents, kv_across))
    dp_count = lax.axis_size("dp")

    def place(g, m):
        return (g // dp_count * mp_count + m) * dp_count + g % dp_count

    mine = lax.ppermute(
        latents,
        ("segment", "mp", "dp"),
        [(place(g, m), place(twice(g) ^ m, m)) for g in range(groups) for m in range(mp_count)],
    )
    kv_across = lax.optimization_barrier((kv_across, mine))[0]
    kv_blocks = dp_blocks(kv_local, kv_across)
    dest = lax.all_to_all(
        jnp.broadcast_to(mine, (mp_count,) + mine.shape), "mp", 0, 0, tiled=True
    ).reshape(LAT * owned, E)

    query = query_matmul(whole_text, text_gain, query_blocks, where)
    dest, query = lax.optimization_barrier((dest, query))
    context, part = attention(
        query, dest, kv_blocks, cotangent[0, 0], frame_counts[0], order, where, jnp.tanh(xgate)
    )

    part = lax.all_to_all(part.reshape(mp_count, share * owned, E), "mp", 0, 0, tiled=True)
    dest_grad = jnp.sum(part.astype(F32), axis=0).astype(BF16)
    cut = groups // share
    send = (
        dest_grad.reshape(share, owned, cut, E // cut)
        .transpose(0, 2, 1, 3)
        .reshape(groups, owned, E // cut)
    )
    send = lax.all_to_all(send, GROUP, 0, 0, tiled=True).reshape(slots, E // cut)
    to_owner = (frame_dest[:, None] == slot_ids[None, :]).astype(BF16)
    send = jnp.dot(to_owner, send, preferred_element_type=F32).astype(BF16)
    send = lax.all_to_all(send.reshape(groups, owned, E // cut), GROUP, 0, 0, tiled=True)
    latent_grad = (
        send.reshape(share, cut, owned, E // cut)
        .transpose(0, 2, 1, 3)
        .reshape(share, owned, E)
        .astype(F32)
    )
    return (context[None, None], latent_grad)


def solution(mesh):
    in_specs = (
        P(("segment", "dp"), "mp", None),
        P(),
        P(),
        P(None, "mp"),
        P(None, None, "mp"),
        P(),
        P("segment", "dp", None, "mp"),
        P("segment", None),
        P("segment", "dp", "mp"),
        P("segment", "dp", None, "mp"),
        P("segment"),
        P("segment", "dp"),
        P(),
        P("segment", "dp", None, "mp"),
    )
    out_specs = (P("segment", "dp", None, "mp"), P("mp", ("segment", "dp"), None))
    return jax.shard_map(
        per_device, mesh=mesh, in_specs=in_specs, out_specs=out_specs, check_vma=False
    )
```

```python
import functools
import math

import jax
import jax.numpy as jnp
from jax import lax
from jax.experimental import pallas as pl
from jax.experimental.pallas import tpu as pltpu
from jax.sharding import PartitionSpec as P

HD = 128
E = 1536
RESAMPLE_HEAD_DIM = 96
PAD = 128
LAT = 64
FMAX = 8
SIDE = 4
GROUP = ("segment", "dp")
BF16 = jnp.bfloat16
F32 = jnp.float32
VMEM_LIMIT = 36 * 1024 * 1024


def layer_norm(inputs, gain_row):
    values = inputs.astype(F32)
    center = values - jnp.mean(values, axis=-1, keepdims=True)
    spread = jnp.mean(center * center, axis=-1, keepdims=True)
    return center * lax.rsqrt(spread + 1e-05) * gain_row.astype(F32)


def shift(value, axis, by):
    pairs = []
    for i in range(SIDE * SIDE):
        y, x = divmod(i, SIDE)
        if axis == "x":
            x = (x + by) % SIDE
        else:
            y = (y + by) % SIDE
        pairs.append((i, y * SIDE + x))
    return lax.ppermute(value, "mp", pairs)


def ring(value, axis):
    half = value.shape[0] // 2
    left = shift(value, axis, 1)
    right = shift(value, axis, -1)
    far = jnp.concatenate([shift(left[:half], axis, 1), shift(right[half:], axis, -1)], axis=0)
    return [value, left, right, far]


def direct(value, axis):
    return [value, shift(value, axis, 1), shift(value, axis, -1), shift(value, axis, 2)]


def twice(k):
    return ((k << 1) ^ ((k >> 3) * 19)) & 15


def halved(k):
    return (k >> 1) ^ ((k & 1) * 9)


def over_z(value):
    return lax.ppermute(value, "dp", [(0, 2), (1, 3), (2, 0), (3, 1)])


def core_swap(value):
    return lax.ppermute(value, "dp", [(0, 1), (1, 0), (2, 3), (3, 2)])


def dp_blocks(value, across):
    return [value, core_swap(value), across, core_swap(across)]


def norm_kernel(value_ref, gains_ref, low_ref, high_ref):
    gain = gains_ref[...].astype(F32)[:1]
    half = low_ref.shape[0]
    low_ref[...] = layer_norm(value_ref[:half, :], gain).astype(BF16)
    high_ref[...] = layer_norm(value_ref[half:, :], gain).astype(BF16)


def norm_halves(value, gains):
    half = jax.ShapeDtypeStruct((value.shape[0] // 2, value.shape[1]), BF16)
    return pl.pallas_call(norm_kernel, out_shape=[half, half])(value, gains)


def resample_kernel(q_ref, lat_ref, *rest):
    pieces, out_ref, held = rest[:-2], rest[-2], rest[-1]
    frames_each = pieces[0].shape[0]
    count = len(pieces) // 4 * frames_each
    q = q_ref[...]
    scale = 1.0 / math.sqrt(RESAMPLE_HEAD_DIM)
    groups = out_ref.shape[0] // count
    share = q.shape[0] // groups
    for f in range(count):
        first = f // frames_each * 4
        blocks = [pieces[first + j][f % frames_each] for j in range(4)]
        pair = jnp.concatenate([lat_ref[...]] + blocks, axis=0)
        score = scale * lax.dot_general(
            q, pair[:, :PAD], (((1,), (1,)), ((), ())), preferred_element_type=F32
        )
        weight = jnp.exp(score - jnp.max(score, axis=1, keepdims=True))
        blend = jnp.dot(weight.astype(BF16), pair[:, PAD:], preferred_element_type=F32)
        blend = blend / jnp.sum(weight, axis=1, keepdims=True)
        for j in range(share):
            to = pl.ds(j * groups * count + f, groups, stride=count)
            held[to, :] = blend[j * groups : (j + 1) * groups]
    for j in range(share):
        rows = slice(j * groups * count, (j + 1) * groups * count)
        out_ref[:, j * PAD : (j + 1) * PAD] = held[rows, :].astype(BF16)


def resample(q, lat_pairs, pieces, slots, share):
    return pl.pallas_call(
        resample_kernel,
        out_shape=jax.ShapeDtypeStruct((slots, share * PAD), BF16),
        scratch_shapes=[pltpu.VMEM((slots * share, PAD), F32)],
    )(q, lat_pairs, *pieces)


def latent_kernel(piece_ref, weight_ref, base_ref, gain_ref, out_ref):
    width = RESAMPLE_HEAD_DIM
    share = piece_ref.shape[1] // PAD
    heads = weight_ref.shape[0] // width
    owned = piece_ref.shape[0] // heads
    piece = piece_ref[...].astype(F32)
    total = base_ref[...]
    for h in range(heads):
        rows = piece[h * owned : (h + 1) * owned]
        left = jnp.concatenate([rows[:, j * PAD : (j + 1) * PAD] for j in range(share)], axis=0)
        total = total + jnp.dot(
            left[:, :width].astype(BF16),
            weight_ref[h * width : (h + 1) * width, :],
            preferred_element_type=F32,
        )
    out_ref[...] = layer_norm(total, gain_ref[...]).astype(BF16)


def latent_rows(piece, weight, base, gain):
    return pl.pallas_call(
        latent_kernel,
        out_shape=jax.ShapeDtypeStruct(base.shape, BF16),
        compiler_params=pltpu.CompilerParams(vmem_limit_bytes=56 * 1024 * 1024),
    )(piece, weight, base, gain)


def query_kernel(where, text_ref, gain_ref, *rest):
    weights = rest[:-5]
    out_ref, held, centered, scale_ref, sems = rest[-5:]
    senders, rows, sent = text_ref.shape
    depth = senders * sent
    group, width = 64, 256
    block = depth // 4
    copies = []
    filled = 0
    for j, weight in enumerate(weights):
        size = weight.shape[0]
        at = where[filled // block] * block + filled % block
        filled += size
        to = held.at[pl.ds(pl.multiple_of(at, 512), size), :]
        copies.append(pltpu.make_async_copy(weight, to, sems.at[j]))
    first = pl.program_id(0) == 0
    each = sent // width

    def chunk(c):
        return c // each, slice(c % each * width, (c % each + 1) * width)

    @pl.when(first)
    def _():
        for copy in copies:
            copy.start()

    @pl.loop(0, rows // group)
    def _(step):
        at = pl.ds(pl.multiple_of(step * group, group), group)
        total = jnp.zeros((group, width), F32)
        for c in range(depth // width):
            total += text_ref[chunk(c)[0], at, chunk(c)[1]].astype(F32)
        mean = jnp.sum(total, axis=1, keepdims=True) * (1.0 / depth)
        square = jnp.zeros((group, width), F32)
        for c in range(depth // width):
            cols = slice(c * width, (c + 1) * width)
            off = text_ref[chunk(c)[0], at, chunk(c)[1]].astype(F32) - mean
            centered[at, cols] = (off * gain_ref[:, cols].astype(F32)).astype(BF16)
            square += off * off
        spread = jnp.sum(square, axis=1, keepdims=True) * (1.0 / depth)
        scale_ref[at, :] = jnp.broadcast_to(lax.rsqrt(spread + 1e-05), (group, 128))

    @pl.when(first)
    def _():
        for copy in copies:
            copy.wait()

    total = jnp.dot(centered[...], held[...], preferred_element_type=F32)
    out_ref[...] = (total * scale_ref[:, :1]).astype(BF16)


def query_matmul(text, gain, weights, where):
    senders, tokens, sent = text.shape
    depth = senders * sent
    cols = weights[0].shape[1]
    rows = 256
    return pl.pallas_call(
        query_kernel,
        grid_spec=pltpu.PrefetchScalarGridSpec(
            num_scalar_prefetch=1,
            grid=(tokens // rows,),
            in_specs=[
                pl.BlockSpec((senders, rows, sent), lambda i, w: (0, i, 0)),
                pl.BlockSpec((1, depth), lambda i, w: (0, 0)),
            ]
            + [pl.BlockSpec(memory_space=pl.ANY) for w in weights],
            out_specs=pl.BlockSpec((rows, cols), lambda i, w: (i, 0)),
            scratch_shapes=[
                pltpu.VMEM((depth, cols), BF16),
                pltpu.VMEM((rows, depth), BF16),
                pltpu.VMEM((rows, 128), F32),
                pltpu.SemaphoreType.DMA((len(weights),)),
            ],
        ),
        out_shape=jax.ShapeDtypeStruct((tokens, cols), BF16),
        compiler_params=pltpu.CompilerParams(vmem_limit_bytes=VMEM_LIMIT),
    )(where, text, gain, *weights)


def attend_kernel(
    count, order, where, gate_ref, q_ref, cot_ref, dest_ref, kv0, kv1, kv2, kv3,
    ctx_ref, part_ref, full, pairs, grads, acc, sems,
):
    tokens = q_ref.shape[0]
    keys = dest_ref.shape[0]
    block = kv0.shape[0]
    rows = 768
    gate = gate_ref[0]
    head = pl.program_id(0)
    heads = pl.num_programs(0)
    cols_k = pl.ds(pl.multiple_of(head * HD, HD), HD)
    cols_v = pl.ds(pl.multiple_of((head + heads) * HD, HD), HD)
    across = (((1,), (1,)), ((), ()))
    down = (((0,), (0,)), ((), ()))

    @pl.when(head == 0)
    def _():
        copies = []
        for j, weight in enumerate((kv0, kv1, kv2, kv3)):
            place = pl.ds(pl.multiple_of(where[j] * block, block), block)
            copies.append(pltpu.make_async_copy(weight, full.at[place, :], sems.at[j]))
        for copy in copies:
            copy.start()
        for copy in copies:
            copy.wait()
        pairs[...] = jnp.dot(dest_ref[...], full[...], preferred_element_type=F32).astype(BF16)

    key = pairs[:, cols_k]
    value = pairs[:, cols_v]
    slot = lax.broadcasted_iota(jnp.int32, (keys, 1), 0) % FMAX
    bias = jnp.where(slot < count[0], 0.0, -1e30)
    scale = 1.0 / math.sqrt(HD)
    for step in range(tokens // rows):
        at = slice(step * rows, (step + 1) * rows)
        q = q_ref[at, :]
        score = lax.dot_general(key, q, across, preferred_element_type=F32) + bias
        top = jnp.max(score, axis=0, keepdims=True)
        weight = jnp.exp((score - top) * scale)
        prob = weight * (1.0 / jnp.sum(weight, axis=0, keepdims=True))
        rounded = prob.astype(BF16)
        blend = lax.dot_general(value, rounded, down, preferred_element_type=F32)
        ctx_ref[at, :] = (gate * blend.T).astype(BF16)
        cot = (gate * cot_ref[at, :].astype(F32)).astype(BF16)
        d_prob = lax.dot_general(value, cot, across, preferred_element_type=F32)
        d_sum = jnp.sum(prob * d_prob, axis=0, keepdims=True)
        d_score = ((d_prob - d_sum) * prob).astype(BF16)
        grad_k = jnp.dot(d_score, q, preferred_element_type=F32)
        grad_v = jnp.dot(rounded, cot, preferred_element_type=F32)
        if step == 0:
            acc[:, :HD] = grad_k
            acc[:, HD:] = grad_v
        else:
            acc[:, :HD] += grad_k
            acc[:, HD:] += grad_v
    chunks = order.shape[0]
    size = keys // chunks
    for j in range(chunks):
        to = pl.ds(pl.multiple_of(order[j] * size, size), size)
        at = slice(j * size, (j + 1) * size)
        grads[to, cols_k] = (acc[at, :HD] * scale).astype(BF16)
        grads[to, cols_v] = acc[at, HD:].astype(BF16)

    @pl.when(head == heads - 1)
    def _():
        part_ref[...] = lax.dot_general(
            grads[...], full[...], across, preferred_element_type=F32
        ).astype(BF16)


def attention(query, dest, kv_blocks, cot, count, order, where, gate):
    tokens, cols = query.shape
    keys, width = dest.shape
    heads = cols // HD
    head = pl.BlockSpec((tokens, HD), lambda h, *_: (0, h))
    whole = lambda a: pl.BlockSpec(a.shape, lambda h, *_: (0, 0), pipeline_mode=pl.Buffered(1))
    return pl.pallas_call(
        attend_kernel,
        grid_spec=pltpu.PrefetchScalarGridSpec(
            num_scalar_prefetch=3,
            grid=(heads,),
            in_specs=[pl.BlockSpec(memory_space=pltpu.SMEM), head, head, whole(dest)]
            + [pl.BlockSpec(memory_space=pl.ANY) for w in kv_blocks],
            out_specs=[head, pl.BlockSpec((keys, width), lambda h, *_: (0, 0))],
            scratch_shapes=[
                pltpu.VMEM((width, 2 * cols), BF16),
                pltpu.VMEM((keys, 2 * cols), BF16),
                pltpu.VMEM((keys, 2 * cols), BF16),
                pltpu.VMEM((keys, 2 * HD), F32),
                pltpu.SemaphoreType.DMA((len(kv_blocks),)),
            ],
        ),
        out_shape=[
            jax.ShapeDtypeStruct((tokens, cols), BF16),
            jax.ShapeDtypeStruct((keys, width), BF16),
        ],
        compiler_params=pltpu.CompilerParams(vmem_limit_bytes=56 * 1024 * 1024),
    )(count, order, where, gate, query, cot, dest, *kv_blocks)


def per_device(
    frames,
    latent_init,
    norm_gains,
    res_query,
    res_kv,
    res_out,
    text,
    text_gain,
    w_query,
    w_kv,
    xgate,
    frame_counts,
    frame_dest,
    cotangent,
):
    mp_count = lax.axis_size("mp")
    group = lax.axis_index(GROUP)
    dp = lax.axis_index("dp")
    share = LAT // mp_count
    slots = frame_dest.shape[0]
    owned = frames.shape[0]
    groups = slots // owned
    width = res_query.shape[1]

    whole_text = lax.all_gather(text[0, 0], "mp", axis=0)
    low, high = norm_halves(frames.reshape(-1, E), norm_gains)
    half_shape = (owned // 2,) + frames.shape[1:]
    phase = [direct(low.reshape(half_shape), "x"), direct(high.reshape(half_shape), "y")]
    joined_halves = [jnp.concatenate(blocks, axis=1) for blocks in phase]
    early = w_query.shape[1] // 4
    low_across = over_z(w_query[0, :early])
    high_across = over_z(w_query[0, early:])
    joined_halves, low_across = lax.optimization_barrier((joined_halves, low_across))
    joined_halves, w_kv = lax.optimization_barrier((joined_halves, w_kv))
    kv_local = jnp.concatenate([w_kv[0, :, 0], w_kv[0, :, 1]], axis=1)

    lat_rows = latent_init.reshape(groups, share, E).swapaxes(0, 1).reshape(LAT, E)
    lat_norm = layer_norm(lat_rows, norm_gains[1]).astype(BF16)
    pad = lambda a: jnp.pad(a, ((0, 0), (0, PAD - width)))
    res_pair = jnp.concatenate([pad(res_kv[:, 0]), pad(res_kv[:, 1])], axis=1)
    res_q = jnp.dot(lat_norm, pad(res_query), preferred_element_type=F32).astype(BF16)
    lat_pairs = jnp.dot(lat_norm, res_pair, preferred_element_type=F32).astype(BF16)
    pieces = []
    for joined, axis in zip(joined_halves, ("y", "x")):
        for block in ring(joined, axis):
            pieces.append(
                jnp.einsum("fpe,ec->fpc", block, res_pair, preferred_element_type=F32).astype(BF16)
            )
    order = halved(group ^ jnp.arange(mp_count, dtype=jnp.int32))
    where = jnp.stack([dp, dp ^ 1, dp ^ 2, dp ^ 3]).astype(jnp.int32)
    pieces, high_across, kv_local, order, where = lax.optimization_barrier(
        (pieces, high_across, kv_local, order, where)
    )
    piece = resample(res_q, lat_pairs, pieces, slots, share)

    piece = lax.all_to_all(
        piece.reshape(groups, owned, share * PAD), GROUP, 0, 0, tiled=True
    ).reshape(slots, share * PAD)
    crossed = (low_across, high_across)
    piece, crossed, kv_local = lax.optimization_barrier((piece, crossed, kv_local))
    query_blocks = [w_query[0], core_swap(w_query[0]), *crossed]
    query_blocks += [core_swap(w) for w in crossed]
    kv_across = over_z(kv_local)
    slot_ids = jnp.arange(slots, dtype=jnp.int32)
    target = (twice(group) ^ (slot_ids // owned)) * owned + slot_ids % owned
    to_dest = (frame_dest[None, :] == target[:, None]).astype(BF16)
    piece = jnp.dot(to_dest, piece, preferred_element_type=F32).astype(BF16)
    piece = lax.all_to_all(
        piece.reshape(mp_count, owned, share * PAD), "mp", 0, 0, tiled=True
    )
    base_rows = lax.dynamic_slice_in_dim(latent_init, group * share, share, 0).astype(F32)
    latents = latent_rows(
        piece.reshape(slots, share * PAD),
        res_out,
        jnp.repeat(base_rows, owned, axis=0),
        norm_gains[2:],
    )
    latents, kv_across, query_blocks = lax.optimization_barrier((latents, kv_across, query_blocks))
    dp_count = lax.axis_size("dp")

    def place(g, m):
        return (g // dp_count * mp_count + m) * dp_count + g % dp_count

    mine = lax.ppermute(
        latents,
        ("segment", "mp", "dp"),
        [(place(g, m), place(twice(g) ^ m, m)) for g in range(groups) for m in range(mp_count)],
    )
    kv_across = lax.optimization_barrier((kv_across, mine))[0]
    kv_blocks = dp_blocks(kv_local, kv_across)
    dest = lax.all_to_all(
        jnp.broadcast_to(mine, (mp_count,) + mine.shape), "mp", 0, 0, tiled=True
    ).reshape(LAT * owned, E)

    query = query_matmul(whole_text, text_gain, query_blocks, where)
    dest, query = lax.optimization_barrier((dest, query))
    context, part = attention(
        query, dest, kv_blocks, cotangent[0, 0], frame_counts[0], order, where, jnp.tanh(xgate)
    )

    part = lax.all_to_all(part.reshape(mp_count, share * owned, E), "mp", 0, 0, tiled=True)
    dest_grad = jnp.sum(part.astype(F32), axis=0).astype(BF16)
    cut = groups // share
    send = (
        dest_grad.reshape(share, owned, cut, E // cut)
        .transpose(0, 2, 1, 3)
        .reshape(groups, owned, E // cut)
    )
    send = lax.all_to_all(send, GROUP, 0, 0, tiled=True).reshape(slots, E // cut)
    to_owner = (frame_dest[:, None] == slot_ids[None, :]).astype(BF16)
    send = jnp.dot(to_owner, send, preferred_element_type=F32).astype(BF16)
    send = lax.all_to_all(send.reshape(groups, owned, E // cut), GROUP, 0, 0, tiled=True)
    latent_grad = (
        send.reshape(share, cut, owned, E // cut)
        .transpose(0, 2, 1, 3)
        .reshape(share, owned, E)
        .astype(F32)
    )
    return (context[None, None], latent_grad)


def solution(mesh):
    in_specs = (
        P(("segment", "dp"), "mp", None),
        P(),
        P(),
        P(None, "mp"),
        P(None, None, "mp"),
        P(),
        P("segment", "dp", None, "mp"),
        P("segment", None),
        P("segment", "dp", "mp"),
        P("segment", "dp", None, "mp"),
        P("segment"),
        P("segment", "dp"),
        P(),
        P("segment", "dp", None, "mp"),
    )
    out_specs = (P("segment", "dp", None, "mp"), P("mp", ("segment", "dp"), None))
    return jax.shard_map(
        per_device, mesh=mesh, in_specs=in_specs, out_specs=out_specs, check_vma=False
    )
```
